512 devices in a mesh: dp: 32 (over y_hi, z, core), tensor: 16 (over x, y_lo).
Axes of the slice: x: 4, y: 8 (y_hi: 2, y_lo: 4; y = y_hi * 4 + y_lo), z: 8, core: 2. Of those that a mesh axis runs over, the one named last changes fastest.
Arguments:
- tokens: bfloat16 [32768, 8192], P('dp', 'tensor'), may hold values from -6 to 6
- value_weight: bfloat16 [8192, 512], P('tensor', 'dp'), may hold values from -0.0625 to 0.0625
- seq_lengths: int32 [32, 3], P('dp'), may hold values from 1 to 512, 1024 in all within a row
- task_ids: int32 [32, 2], replicated, may hold values from 0 to 31
- task_embed: bfloat16 [32, 1024], replicated, may hold values from -6 to 6
- hyper_in: bfloat16 [1024, 512], P(None, 'dp'), may hold values from -0.1875 to 0.1875
- head_a: bfloat16 [512, 65536], P('dp', 'tensor'), may hold values from -0.25 to 0.25
- head_b: bfloat16 [512, 4096], P('dp', 'tensor'), may hold values from -0.25 to 0.25
- cotangent: bfloat16 [32768, 512], P(('dp', 'tensor')), may hold values from -6 to 6
Outputs:
- values: bfloat16 [32768, 512], P(('dp', 'tensor'))
- grad_tokens: bfloat16 [32768, 8192], P('dp', 'tensor')
- grad_head_a: float32 [512, 65536], P('dp', 'tensor')
- grad_head_b: float32 [512, 4096], P('dp', 'tensor')
- grad_hyper_in: float32 [1024, 512], P(None, 'dp')
The draws below stay inside these ranges and needn't reach their ends.
Inputs may be any that keep to these rules, and one draw needn't show every extreme that they name: `seq_lengths`: each row lists a group's 2 task batch lengths in order and then its count of padding rows; each row sums to 1024 and its largest entry is exactly 512.
All inputs are finite; a program needn't handle non-finite values.
Results may differ from the reference program's by a relative error of at most 0.0065.
Values may be sent and summed in bfloat16 or wider, within the bound.
No kernel may reach another device: no remote copies, remote signals or barrier semaphores. Data moves between devices by JAX's collectives and lax.ppermute only.
A program may use at most 64 MiB of HBM per device.

```python
import math
import jax
import jax.numpy as jnp
import numpy as np
from jax import lax

D = 8192
KV = 512
R = 8
E = 1024
H = 512
NTASK = 32
SEQS = 2
TOK_DEV = 1024
TOKENS = 32768
N_DP = 32


def plant(drawn, own_key, least, top_value):
    place = [jax.random.randint(jax.random.fold_in(own_key, axis), (), 0, length) for axis, length in enumerate(drawn.shape)]
    widest = drawn.shape.index(max(drawn.shape))
    neighbour = place[:widest] + [(place[widest] + 1) % drawn.shape[widest]] + place[widest + 1:]
    return drawn.at[tuple(place)].set(least).at[tuple(neighbour)].set(top_value)


def block_scale(own_key, dims, split, smallest, largest):
    def one(dim, blocks):
        draws = jax.random.uniform(jax.random.fold_in(jax.random.fold_in(own_key, 6), dim), (blocks,), jnp.float32, smallest / len(split), largest / len(split))
        return jnp.repeat(jnp.exp(draws), dims[dim] // blocks).reshape((-1,) + (1,) * (len(dims) - dim - 1))

    gain = one(*split[0])
    for cut in split[1:]:
        gain = gain * one(*cut)
    return gain


def split_up(amount, total, most, skew):
    portions = [(1 << 20) // math.isqrt(rank ** skew) + 1 for rank in range(2, amount + 1)]
    spare, given = total - most - (amount - 1), [1] * (amount - 1)
    while spare > 0:
        free = [i for i in range(amount - 1) if given[i] < most]
        pool, budget = sum([portions[i] for i in free]), spare
        for i in free:
            addition = min(most - given[i], max(1, budget * portions[i] // pool), spare)
            given[i] = given[i] + addition
            spare = spare - addition
    return np.array([most] + given)


def ragged_sizes(key, amount, total, bound, skew):
    if amount == 2:
        one = jax.random.randint(key, (), max(1, total - bound), min(bound, total - 1) + 1)
        return jnp.stack([one, total - one])
    tallies = jnp.asarray(split_up(amount, total, bound, skew), jnp.int32)
    couples = (amount - 1) // 2
    giver, taker = tallies[1:1 + 2 * couples:2], tallies[2:2 + 2 * couples:2]
    room = jnp.minimum(giver - 1, bound - taker)
    passed = jax.random.randint(jax.random.fold_in(key, 1), (couples,), 0, 1 << 20) % (room + 1)
    tallies = tallies.at[1:1 + 2 * couples:2].set(giver - passed).at[2:2 + 2 * couples:2].set(taker + passed)
    return tallies[jax.random.permutation(jax.random.fold_in(key, 2), amount)]


def normal_values(key, shape, spread, most, pieces=(), kind=jnp.bfloat16):
    loudness = block_scale(key, shape, pieces, -0.22, 0.18) if pieces else 1.0
    drawn = jax.random.normal(key, shape, jnp.float32) * spread * loudness
    return jnp.minimum(jnp.maximum(drawn, -most), most).astype(kind)


def setup_inputs(seed: int = 0) -> dict:
    key_of = jax.random.split(jax.random.key(seed), 10)
    tokens = normal_values(key_of[0], (TOKENS, D), 1.0, 6.0, ((0, 32), (1, 16)))
    value_weight = normal_values(key_of[1], (D, KV), D ** -0.5, 0.0625, ((0, 16), (1, 32)))
    seq_lengths = jax.vmap(lambda own: ragged_sizes(own, SEQS + 1, TOK_DEV, TOK_DEV // 2, 2))(jax.random.split(key_of[2], N_DP)).reshape((N_DP, SEQS + 1)).astype(jnp.int32)
    task_ids = plant(jax.random.randint(key_of[3], (N_DP, SEQS), 0, NTASK), jax.random.fold_in(key_of[3], 1), 0, NTASK - 1).astype(jnp.int32)
    task_embed = normal_values(key_of[4], (NTASK, E), 1.0, 6.0)
    hyper_in = normal_values(key_of[5], (E, H), E ** -0.5, 0.1875, ((1, 32),))
    head_a = normal_values(key_of[6], (H, D * R), H ** -0.5, 0.25, ((0, 32), (1, 16)))
    head_b = normal_values(key_of[7], (H, KV * R), H ** -0.5, 0.25, ((0, 32), (1, 16)))
    cotangent = normal_values(key_of[8], (TOKENS, KV), 1.0, 6.0, ((0, 512),))
    return dict(tokens=tokens, value_weight=value_weight, seq_lengths=seq_lengths, task_ids=task_ids, task_embed=task_embed, hyper_in=hyper_in, head_a=head_a, head_b=head_b, cotangent=cotangent)


precise = lax.Precision.HIGHEST

def silu_slope(pre_act):
    sigma = jax.nn.sigmoid(pre_act)
    return sigma * (1.0 + pre_act * (1.0 - sigma))

def membership(lengths):
    finish = jnp.cumsum(lengths)
    anchor = finish - lengths
    places = jnp.arange(TOK_DEV, dtype=jnp.int32)[:, None]
    inside = (places >= anchor[None, :SEQS]) & (places < finish[None, :SEQS])
    return jnp.repeat(inside.astype(jnp.float32), R, axis=1)

def reference(tokens, value_weight, seq_lengths, task_ids, task_embed, hyper_in, head_a, head_b, cotangent):
    pre_act = jnp.dot(task_embed, hyper_in, preferred_element_type=jnp.float32)
    hidden = jax.nn.silu(pre_act).astype(jnp.bfloat16)
    adapt_down = (jnp.dot(hidden, head_a, preferred_element_type=jnp.float32) * (1.0 / math.sqrt(D))).astype(jnp.bfloat16)
    adapt_up = (jnp.dot(hidden, head_b, preferred_element_type=jnp.float32) * (1.0 / math.sqrt(R))).astype(jnp.bfloat16)

    def group_pass(inputs):
        rows_x, rows_g, lengths, chosen = inputs
        col_mask = membership(lengths)
        down_cat = adapt_down[chosen].reshape(SEQS, D, R).transpose(1, 0, 2).reshape(D, SEQS * R)
        up_cat = adapt_up[chosen].reshape(SEQS, KV, R).transpose(1, 0, 2).reshape(KV, SEQS * R)
        frozen = jnp.dot(rows_x, value_weight, preferred_element_type=jnp.float32)
        low_rank = jnp.dot(rows_x, down_cat, preferred_element_type=jnp.float32) * col_mask
        adapter = jnp.dot(low_rank, up_cat.astype(jnp.float32).T, precision=precise)
        values = (frozen + adapter).astype(jnp.bfloat16)
        back_low = (jnp.dot(rows_g, up_cat, preferred_element_type=jnp.float32) * col_mask).astype(jnp.bfloat16)
        grad_rows = jnp.dot(rows_g, value_weight.T, preferred_element_type=jnp.float32)
        grad_rows = (grad_rows + jnp.dot(back_low, down_cat.T, preferred_element_type=jnp.float32)).astype(jnp.bfloat16)
        down_grad = jnp.dot(rows_x.T, back_low, preferred_element_type=jnp.float32)
        up_grad = jnp.dot(rows_g.astype(jnp.float32).T, low_rank, precision=precise)
        down_seq = down_grad.reshape(D, SEQS, R).transpose(1, 0, 2).reshape(SEQS, D * R)
        up_seq = up_grad.reshape(KV, SEQS, R).transpose(1, 0, 2).reshape(SEQS, KV * R)
        return (values, grad_rows, down_seq, up_seq)
    values, grad_tokens, down_seq, up_seq = lax.map(group_pass, (tokens.reshape(N_DP, TOK_DEV, D), cotangent.reshape(N_DP, TOK_DEV, KV), seq_lengths, task_ids))
    values = values.reshape(N_DP * TOK_DEV, KV)
    grad_tokens = grad_tokens.reshape(N_DP * TOK_DEV, D)
    one_hot = (task_ids.reshape(-1)[:, None] == jnp.arange(NTASK, dtype=jnp.int32)[None, :]).astype(jnp.float32)
    down_task = jnp.dot(one_hot.T, down_seq.reshape(N_DP * SEQS, D * R), precision=precise) * (1.0 / math.sqrt(D))
    up_task = jnp.dot(one_hot.T, up_seq.reshape(N_DP * SEQS, KV * R), precision=precise) * (1.0 / math.sqrt(R))
    hidden_wide = hidden.astype(jnp.float32)
    grad_head_a = jnp.dot(hidden_wide.T, down_task, precision=precise)
    grad_head_b = jnp.dot(hidden_wide.T, up_task, precision=precise)
    grad_hidden = jnp.dot(down_task, head_a.astype(jnp.float32).T, precision=precise)
    grad_hidden = grad_hidden + jnp.dot(up_task, head_b.astype(jnp.float32).T, precision=precise)
    grad_pre = grad_hidden * silu_slope(pre_act)
    grad_hyper_in = jnp.dot(task_embed.astype(jnp.float32).T, grad_pre, precision=precise)
    return (values, grad_tokens, grad_head_a, grad_head_b, grad_hyper_in)
```

```python
import math

import jax
import jax.numpy as jnp
from jax import lax
from jax.sharding import PartitionSpec as P

D = 8192
KV = 512
R = 8
NTASK = 32
SEQS = 2
ADA = SEQS * R

precise = lax.Precision.HIGHEST
inner_dims = (((1,), (1,)), ((), ()))
outer_dims = (((0,), (0,)), ((), ()))
bf16 = jnp.bfloat16
f32 = jnp.float32

Y_RUN = 4


def silu_slope(pre_act):
    sigma = jax.nn.sigmoid(pre_act)
    return sigma * (1.0 + pre_act * (1.0 - sigma))


def spread(block, axes, count, **kw):
    copies = jnp.broadcast_to(block[None], (count,) + block.shape)
    return lax.all_to_all(copies, axes, 0, 0, **kw)


def shards(
    tokens, value_weight, seq_lengths, task_ids, task_embed, hyper_in, head_a, head_b, cotangent
):
    n_dp = lax.axis_size("dp")
    n_tensor = lax.axis_size("tensor")
    n_x = n_tensor // Y_RUN
    rows_total, width_own = tokens.shape
    rows_own = rows_total // n_tensor
    outputs_own = KV // n_tensor
    along_y = [[x * Y_RUN + y for y in range(Y_RUN)] for x in range(n_x)]
    along_x = [[x * Y_RUN + y for x in range(n_x)] for y in range(Y_RUN)]

    weight_t = spread(value_weight.T, "dp", n_dp).reshape(KV, width_own)

    cot_run = spread(cotangent, "tensor", Y_RUN, axis_index_groups=along_y)
    cot_full = spread(
        cot_run.reshape(Y_RUN * rows_own, KV), "tensor", n_x, axis_index_groups=along_x
    ).reshape(rows_total, KV)

    pre_act = jnp.dot(task_embed, hyper_in, preferred_element_type=f32)
    hidden = jax.nn.silu(pre_act).astype(bf16)
    every_id = task_ids.reshape(n_dp * SEQS)
    one_hot = (every_id[:, None] == jnp.arange(NTASK, dtype=jnp.int32)[None, :]).astype(bf16)
    hidden_pick = jnp.dot(one_hot, hidden, preferred_element_type=f32).astype(bf16)
    terms = jnp.concatenate(
        (
            jnp.dot(hidden_pick, head_a, preferred_element_type=f32),
            jnp.dot(hidden_pick, head_b, preferred_element_type=f32),
        ),
        axis=1,
    ).astype(bf16)
    down_width = width_own * R
    up_width = outputs_own * R
    sums = jnp.sum(
        lax.all_to_all(terms.reshape(n_dp, SEQS, -1), "dp", 0, 0).astype(f32), axis=0
    )
    down_pick = (sums[:, :down_width] * (1.0 / math.sqrt(D))).astype(bf16)
    up_pick = (sums[:, down_width:] * (1.0 / math.sqrt(R))).astype(bf16)
    down_cat = down_pick.reshape(SEQS, width_own, R).transpose(1, 0, 2).reshape(width_own, ADA)

    lengths = seq_lengths[0]
    finish = jnp.cumsum(lengths)
    anchor = finish - lengths
    places = jnp.arange(rows_total, dtype=jnp.int32)[:, None]
    inside = (places >= anchor[None, :SEQS]) & (places < finish[None, :SEQS])
    col_mask = jnp.repeat(inside.astype(f32), R, axis=1)

    frozen = lax.dot_general(tokens, weight_t, inner_dims, preferred_element_type=f32).astype(bf16)
    low_part = (jnp.dot(tokens, down_cat, preferred_element_type=f32) * col_mask).astype(bf16)
    up_part = lax.dot_general(cot_full, low_part, outer_dims, preferred_element_type=f32).astype(
        bf16
    )
    low_lines = rows_own * ADA // KV
    up_lines = outputs_own * ADA // KV
    pick_lines = SEQS * up_width // KV
    block = jnp.concatenate(
        (
            frozen.reshape(n_tensor, rows_own, KV),
            low_part.reshape(n_tensor, low_lines, KV),
            up_part.reshape(n_tensor, up_lines, KV),
            jnp.broadcast_to(up_pick.reshape(1, pick_lines, KV), (n_tensor, pick_lines, KV)),
        ),
        axis=1,
    ).reshape(n_x, Y_RUN, -1, KV)
    summed = rows_own + low_lines + up_lines
    from_x = lax.all_to_all(block, "tensor", 0, 0, axis_index_groups=along_x)
    x_sums = jnp.sum(from_x[:, :, :summed].astype(f32), axis=0).astype(bf16)
    x_picks = from_x[:, :, summed:].transpose(1, 0, 2, 3).reshape(Y_RUN, n_x * pick_lines, KV)
    from_y = lax.all_to_all(
        jnp.concatenate((x_sums, x_picks), axis=1), "tensor", 0, 0, axis_index_groups=along_y
    )
    whole = jnp.sum(from_y[:, :summed].astype(f32), axis=0)
    frozen_rows = whole[:rows_own]
    low_rows = whole[rows_own : rows_own + low_lines].reshape(rows_own, ADA)
    up_grad = whole[rows_own + low_lines :].reshape(outputs_own, ADA)
    up_cat = (
        from_y[:, summed:]
        .reshape(Y_RUN, n_x, SEQS, outputs_own, R)
        .transpose(1, 0, 3, 2, 4)
        .reshape(KV, ADA)
    )

    back_low = (jnp.dot(cot_full, up_cat, preferred_element_type=f32) * col_mask).astype(bf16)
    down_grad = lax.dot_general(tokens, back_low, outer_dims, preferred_element_type=f32)
    down_seq = down_grad.reshape(width_own, SEQS, R).transpose(1, 0, 2).reshape(SEQS, down_width)
    up_seq = up_grad.reshape(outputs_own, SEQS, R).transpose(1, 0, 2).reshape(SEQS, up_width)
    grads = spread(
        jnp.concatenate((down_seq, up_seq), axis=1).astype(bf16), "dp", n_dp
    ).reshape(n_dp * SEQS, -1)
    down_all = grads[:, :down_width]
    up_all = grads[:, down_width:]

    down_scale = 1.0 / math.sqrt(D)
    up_scale = 1.0 / math.sqrt(R)
    hidden_part = lax.dot_general(down_all, head_a, inner_dims, preferred_element_type=f32)
    hidden_part = hidden_part * down_scale + up_scale * lax.dot_general(
        up_all, head_b, inner_dims, preferred_element_type=f32
    )
    by_task = lax.dot_general(
        one_hot.astype(f32), hidden_part, outer_dims, precision=precise
    )
    grad_hidden = jnp.sum(spread(by_task, "tensor", n_tensor), axis=0)
    grad_head_a = down_scale * lax.dot_general(
        hidden_pick, down_all, outer_dims, preferred_element_type=f32
    )
    grad_head_b = up_scale * lax.dot_general(
        hidden_pick, up_all, outer_dims, preferred_element_type=f32
    )
    grad_pre = grad_hidden * silu_slope(pre_act)
    grad_hyper_in = lax.dot_general(
        task_embed.astype(f32), grad_pre, outer_dims, precision=precise
    )

    adapter = lax.dot_general(
        low_rows.astype(f32), up_cat.astype(f32), inner_dims, precision=precise
    )
    values = (frozen_rows + adapter).astype(bf16)
    adapter_back = lax.dot_general(back_low, down_cat, inner_dims, preferred_element_type=f32)
    frozen_back = jnp.dot(cot_full, weight_t, preferred_element_type=f32)
    grad_tokens = (frozen_back + adapter_back).astype(bf16)
    return (values, grad_tokens, grad_head_a, grad_head_b, grad_hyper_in)


def solution(mesh):
    placed = (
        P("dp", "tensor"),
        P("tensor", "dp"),
        P("dp", None),
        P(),
        P(),
        P(None, "dp"),
        P("dp", "tensor"),
        P("dp", "tensor"),
        P(("dp", "tensor"), None),
    )
    return jax.shard_map(
        shards,
        mesh=mesh,
        in_specs=placed,
        out_specs=(
            P(("dp", "tensor"), None),
            P("dp", "tensor"),
            P("dp", "tensor"),
            P("dp", "tensor"),
            P(None, "dp"),
        ),
        check_vma=False,
    )
```

```python
import math

import jax
import jax.numpy as jnp
from jax import lax
from jax.sharding import PartitionSpec as P

D = 8192
KV = 512
R = 8
NTASK = 32
SEQS = 2
ADA = SEQS * R

precise = lax.Precision.HIGHEST
inner_dims = (((1,), (1,)), ((), ()))
outer_dims = (((0,), (0,)), ((), ()))
bf16 = jnp.bfloat16
f32 = jnp.float32

Y_RUN = 4


def silu_slope(pre_act):
    sigma = jax.nn.sigmoid(pre_act)
    return sigma * (1.0 + pre_act * (1.0 - sigma))


def spread(block, axes, count, **kw):
    copies = jnp.broadcast_to(block[None], (count,) + block.shape)
    return lax.all_to_all(copies, axes, 0, 0, **kw)


def gathered(block, part, count, stride, total):
    every = jnp.zeros((count,) + block.shape, block.dtype)
    every = lax.dynamic_update_index_in_dim(every, block, part, 0)
    for step in range(1, count):
        pairs = [(i, i ^ (step * stride)) for i in range(total)]
        other = lax.ppermute(block, "tensor", pairs)
        every = lax.dynamic_update_index_in_dim(every, other, part ^ step, 0)
    return every.reshape((count * block.shape[0],) + block.shape[1:])


def shards(
    tokens, value_weight, seq_lengths, task_ids, task_embed, hyper_in, head_a, head_b, cotangent
):
    n_dp = lax.axis_size("dp")
    n_tensor = lax.axis_size("tensor")
    n_x = n_tensor // Y_RUN
    rows_total, width_own = tokens.shape
    rows_own = rows_total // n_tensor
    outputs_own = KV // n_tensor
    along_y = [[x * Y_RUN + y for y in range(Y_RUN)] for x in range(n_x)]
    along_x = [[x * Y_RUN + y for x in range(n_x)] for y in range(Y_RUN)]

    place = lax.axis_index("tensor")
    cot_run = gathered(cotangent, place % Y_RUN, Y_RUN, 1, n_tensor)
    cot_full = gathered(cot_run, place // Y_RUN, n_x, Y_RUN, n_tensor)

    pre_act = jnp.dot(task_embed, hyper_in, preferred_element_type=f32)
    hidden = jax.nn.silu(pre_act).astype(bf16)
    every_id = task_ids.reshape(n_dp * SEQS)
    one_hot = (every_id[:, None] == jnp.arange(NTASK, dtype=jnp.int32)[None, :]).astype(bf16)
    hidden_pick = jnp.dot(one_hot, hidden, preferred_element_type=f32).astype(bf16)
    terms = jnp.concatenate(
        (
            jnp.dot(hidden_pick, head_a, preferred_element_type=f32),
            jnp.dot(hidden_pick, head_b, preferred_element_type=f32),
        ),
        axis=1,
    ).astype(bf16)
    down_width = width_own * R
    up_width = outputs_own * R
    weight_own = value_weight.T
    term_lines = SEQS * (down_width + up_width) // width_own
    sent = jnp.concatenate(
        (
            terms.reshape(n_dp, term_lines, width_own),
            jnp.broadcast_to(weight_own[None], (n_dp,) + weight_own.shape),
        ),
        axis=1,
    )
    came = lax.all_to_all(sent, "dp", 0, 0)
    weight_t = came[:, term_lines:].reshape(KV, width_own)
    sums = jnp.sum(came[:, :term_lines].astype(f32), axis=0).reshape(SEQS, -1)
    down_pick = (sums[:, :down_width] * (1.0 / math.sqrt(D))).astype(bf16)
    up_pick = (sums[:, down_width:] * (1.0 / math.sqrt(R))).astype(bf16)
    down_cat = down_pick.reshape(SEQS, width_own, R).transpose(1, 0, 2).reshape(width_own, ADA)

    lengths = seq_lengths[0]
    finish = jnp.cumsum(lengths)
    anchor = finish - lengths
    places = jnp.arange(rows_total, dtype=jnp.int32)[:, None]
    inside = (places >= anchor[None, :SEQS]) & (places < finish[None, :SEQS])
    col_mask = jnp.repeat(inside.astype(f32), R, axis=1)

    frozen = lax.dot_general(tokens, weight_t, inner_dims, preferred_element_type=f32)
    frozen_rows = lax.psum_scatter(
        frozen.reshape(n_x, Y_RUN * rows_own, KV),
        "tensor",
        scatter_dimension=0,
        axis_index_groups=along_x,
    )
    frozen_rows = lax.psum_scatter(
        frozen_rows.reshape(Y_RUN, rows_own, KV),
        "tensor",
        scatter_dimension=0,
        axis_index_groups=along_y,
    )
    low_part = (jnp.dot(tokens, down_cat, preferred_element_type=f32) * col_mask).astype(bf16)
    up_part = lax.dot_general(cot_full, low_part, outer_dims, preferred_element_type=f32).astype(
        bf16
    )
    low_lines = rows_own * ADA // KV
    up_lines = outputs_own * ADA // KV
    pick_lines = SEQS * up_width // KV
    block = jnp.concatenate(
        (
            low_part.reshape(n_tensor, low_lines, KV),
            up_part.reshape(n_tensor, up_lines, KV),
            jnp.broadcast_to(up_pick.reshape(1, pick_lines, KV), (n_tensor, pick_lines, KV)),
        ),
        axis=1,
    )
    summed = low_lines + up_lines
    came = lax.all_to_all(block, "tensor", 0, 0)
    whole = jnp.sum(came[:, :summed].astype(f32), axis=0)
    low_rows = whole[:low_lines].reshape(rows_own, ADA)
    up_grad = whole[low_lines:].reshape(outputs_own, ADA)
    up_cat = (
        came[:, summed:]
        .reshape(n_tensor, SEQS, outputs_own, R)
        .transpose(0, 2, 1, 3)
        .reshape(KV, ADA)
    )

    back_low = (jnp.dot(cot_full, up_cat, preferred_element_type=f32) * col_mask).astype(bf16)
    down_grad = lax.dot_general(tokens, back_low, outer_dims, preferred_element_type=f32)
    down_seq = down_grad.reshape(width_own, SEQS, R).transpose(1, 0, 2).reshape(SEQS, down_width)
    up_seq = up_grad.reshape(outputs_own, SEQS, R).transpose(1, 0, 2).reshape(SEQS, up_width)
    grads = spread(
        jnp.concatenate((down_seq, up_seq), axis=1).astype(bf16), "dp", n_dp
    ).reshape(n_dp * SEQS, -1)
    down_all = grads[:, :down_width]
    up_all = grads[:, down_width:]

    down_scale = 1.0 / math.sqrt(D)
    up_scale = 1.0 / math.sqrt(R)
    hidden_part = lax.dot_general(down_all, head_a, inner_dims, preferred_element_type=f32)
    hidden_part = hidden_part * down_scale + up_scale * lax.dot_general(
        up_all, head_b, inner_dims, preferred_element_type=f32
    )
    by_task = lax.dot_general(
        one_hot.astype(f32), hidden_part, outer_dims, precision=precise
    )
    grad_hidden = jnp.sum(spread(by_task, "tensor", n_tensor), axis=0)
    grad_head_a = down_scale * lax.dot_general(
        hidden_pick, down_all, outer_dims, preferred_element_type=f32
    )
    grad_head_b = up_scale * lax.dot_general(
        hidden_pick, up_all, outer_dims, preferred_element_type=f32
    )
    grad_pre = grad_hidden * silu_slope(pre_act)
    grad_hyper_in = lax.dot_general(
        task_embed.astype(f32), grad_pre, outer_dims, precision=precise
    )

    adapter = lax.dot_general(
        low_rows.astype(f32), up_cat.astype(f32), inner_dims, precision=precise
    )
    values = (frozen_rows + adapter).astype(bf16)
    adapter_back = lax.dot_general(back_low, down_cat, inner_dims, preferred_element_type=f32)
    frozen_back = jnp.dot(cot_full, weight_t, preferred_element_type=f32)
    grad_tokens = (frozen_back + adapter_back).astype(bf16)
    return (values, grad_tokens, grad_head_a, grad_head_b, grad_hyper_in)


def solution(mesh):
    placed = (
        P("dp", "tensor"),
        P("tensor", "dp"),
        P("dp", None),
        P(),
        P(),
        P(None, "dp"),
        P("dp", "tensor"),
        P("dp", "tensor"),
        P(("dp", "tensor"), None),
    )
    return jax.shard_map(
        shards,
        mesh=mesh,
        in_specs=placed,
        out_specs=(
            P(("dp", "tensor"), None),
            P("dp", "tensor"),
            P("dp", "tensor"),
            P("dp", "tensor"),
            P(None, "dp"),
        ),
        check_vma=False,
    )
```

```python
import math

import jax
import jax.numpy as jnp
from jax import lax
from jax.sharding import PartitionSpec as P

D = 8192
KV = 512
R = 8
NTASK = 32
SEQS = 2
ADA = SEQS * R

precise = lax.Precision.HIGHEST
inner_dims = (((1,), (1,)), ((), ()))
outer_dims = (((0,), (0,)), ((), ()))
bf16 = jnp.bfloat16
f32 = jnp.float32

CORES = 2
Y_RUN = 4


def silu_slope(pre_act):
    sigma = jax.nn.sigmoid(pre_act)
    return sigma * (1.0 + pre_act * (1.0 - sigma))


def spread(block, axes, count, **kw):
    copies = jnp.broadcast_to(block[None], (count,) + block.shape)
    return lax.all_to_all(copies, axes, 0, 0, **kw)


def swapped(block, axis, distance):
    pairs = [(i, i ^ distance) for i in range(lax.axis_size(axis))]
    return lax.ppermute(block, axis, pairs)


def gathered(block, part, count, stride):
    every = jnp.zeros((count,) + block.shape, block.dtype)
    every = lax.dynamic_update_index_in_dim(every, block, part, 0)
    for step in range(1, count):
        other = swapped(block, "tensor", step * stride)
        every = lax.dynamic_update_index_in_dim(every, other, part ^ step, 0)
    return every.reshape((count * block.shape[0],) + block.shape[1:])


def summed_rows(rows, place, total):
    distance = total // 2
    while distance:
        halves = rows.reshape((2, rows.shape[0] // 2) + rows.shape[1:])
        bit = (place // distance) % 2
        kept = lax.dynamic_index_in_dim(halves, bit, 0, keepdims=False)
        given = lax.dynamic_index_in_dim(halves, 1 - bit, 0, keepdims=False)
        other = swapped(given, "tensor", distance)
        rows = kept.astype(f32) + other.astype(f32)
        distance //= 2
        if distance:
            rows = rows.astype(bf16)
    return rows


def shards(
    tokens, value_weight, seq_lengths, task_ids, task_embed, hyper_in, head_a, head_b, cotangent
):
    n_dp = lax.axis_size("dp")
    n_chips = n_dp // CORES
    n_tensor = lax.axis_size("tensor")
    n_x = n_tensor // Y_RUN
    rows_total, width_own = tokens.shape
    rows_own = rows_total // n_tensor
    outputs_own = KV // n_tensor
    down_width = width_own * R
    up_width = outputs_own * R
    same_core = [[chip * CORES + core for chip in range(n_chips)] for core in range(CORES)]
    core = lax.axis_index("dp") % CORES
    place = lax.axis_index("tensor")

    pre_act = jnp.dot(task_embed, hyper_in, preferred_element_type=f32)
    hidden = jax.nn.silu(pre_act).astype(bf16)

    def chosen_by(which):
        ids = lax.dynamic_index_in_dim(
            task_ids.reshape(n_chips, CORES, SEQS), which, 1, keepdims=False
        ).reshape(n_chips * SEQS)
        hot = (ids[:, None] == jnp.arange(NTASK, dtype=jnp.int32)[None, :]).astype(bf16)
        return hot, jnp.dot(hot, hidden, preferred_element_type=f32).astype(bf16)

    def terms_of(pick):
        return jnp.concatenate(
            (
                jnp.dot(pick, head_a, preferred_element_type=f32),
                jnp.dot(pick, head_b, preferred_element_type=f32),
            ),
            axis=1,
        )

    hot_mate, pick_mate = chosen_by(1 - core)
    hot_mine, pick_mine = chosen_by(core)
    from_mate = swapped(terms_of(pick_mate).astype(bf16), "dp", 1)
    terms = (terms_of(pick_mine) + from_mate.astype(f32)).astype(bf16)
    weight_own = value_weight.T
    term_lines = SEQS * (down_width + up_width) // width_own
    sent = jnp.concatenate(
        (
            terms.reshape(n_chips, term_lines, width_own),
            jnp.broadcast_to(weight_own[None], (n_chips,) + weight_own.shape),
        ),
        axis=1,
    )
    came = lax.all_to_all(sent, "dp", 0, 0, axis_index_groups=same_core)
    sums = jnp.sum(came[:, :term_lines].astype(f32), axis=0).reshape(SEQS, -1)
    down_pick = (sums[:, :down_width] * (1.0 / math.sqrt(D))).astype(bf16)
    up_pick = (sums[:, down_width:] * (1.0 / math.sqrt(R))).astype(bf16)
    down_cat = down_pick.reshape(SEQS, width_own, R).transpose(1, 0, 2).reshape(width_own, ADA)

    cot_run = gathered(cotangent, place % Y_RUN, Y_RUN, 1)
    cot_full = gathered(cot_run, place // Y_RUN, n_x, Y_RUN)

    lengths = seq_lengths[0]
    finish = jnp.cumsum(lengths)
    anchor = finish - lengths
    places = jnp.arange(rows_total, dtype=jnp.int32)[:, None]
    inside = (places >= anchor[None, :SEQS]) & (places < finish[None, :SEQS])
    col_mask = jnp.repeat(inside.astype(f32), R, axis=1)

    low_part = (jnp.dot(tokens, down_cat, preferred_element_type=f32) * col_mask).astype(bf16)
    up_part = lax.dot_general(cot_full, low_part, outer_dims, preferred_element_type=f32).astype(
        bf16
    )
    low_lines = rows_own * ADA // KV
    up_lines = outputs_own * ADA // KV
    pick_lines = SEQS * up_width // KV
    block = jnp.concatenate(
        (
            low_part.reshape(n_tensor, low_lines, KV),
            up_part.reshape(n_tensor, up_lines, KV),
            jnp.broadcast_to(up_pick.reshape(1, pick_lines, KV), (n_tensor, pick_lines, KV)),
        ),
        axis=1,
    )
    summed = low_lines + up_lines
    low_came = lax.all_to_all(block, "tensor", 0, 0)
    whole = jnp.sum(low_came[:, :summed].astype(f32), axis=0)
    low_rows = whole[:low_lines].reshape(rows_own, ADA)
    up_grad = whole[low_lines:].reshape(outputs_own, ADA)
    up_cat = (
        low_came[:, summed:]
        .reshape(n_tensor, SEQS, outputs_own, R)
        .transpose(0, 2, 1, 3)
        .reshape(KV, ADA)
    )

    weight_mine = came[:, term_lines:]
    weight_mate = swapped(weight_mine, "dp", 1)
    weight_t = jnp.stack(
        (
            jnp.where(core == 0, weight_mine, weight_mate),
            jnp.where(core == 0, weight_mate, weight_mine),
        ),
        axis=1,
    ).reshape(KV, width_own)
    frozen = lax.dot_general(tokens, weight_t, inner_dims, preferred_element_type=f32).astype(bf16)
    frozen_rows = summed_rows(frozen, place, n_tensor)

    back_low = (jnp.dot(cot_full, up_cat, preferred_element_type=f32) * col_mask).astype(bf16)
    down_grad = lax.dot_general(tokens, back_low, outer_dims, preferred_element_type=f32)
    down_seq = down_grad.reshape(width_own, SEQS, R).transpose(1, 0, 2).reshape(SEQS, down_width)
    up_seq = up_grad.reshape(outputs_own, SEQS, R).transpose(1, 0, 2).reshape(SEQS, up_width)
    grads_mine = spread(
        jnp.concatenate((down_seq, up_seq), axis=1).astype(bf16),
        "dp",
        n_chips,
        axis_index_groups=same_core,
    )
    grads_mate = swapped(grads_mine, "dp", 1)

    down_scale = 1.0 / math.sqrt(D)
    up_scale = 1.0 / math.sqrt(R)

    def head_terms(grads, pick, hot):
        rows = grads.reshape(n_chips * SEQS, -1)
        down_rows = rows[:, :down_width]
        up_rows = rows[:, down_width:]
        part = down_scale * lax.dot_general(
            down_rows, head_a, inner_dims, preferred_element_type=f32
        ) + up_scale * lax.dot_general(up_rows, head_b, inner_dims, preferred_element_type=f32)
        return (
            lax.dot_general(hot.astype(f32), part, outer_dims, precision=precise),
            lax.dot_general(pick, down_rows, outer_dims, preferred_element_type=f32),
            lax.dot_general(pick, up_rows, outer_dims, preferred_element_type=f32),
        )

    of_mine = head_terms(grads_mine, pick_mine, hot_mine)
    of_mate = head_terms(grads_mate, pick_mate, hot_mate)
    by_task = of_mine[0] + of_mate[0]
    grad_head_a = down_scale * (of_mine[1] + of_mate[1])
    grad_head_b = up_scale * (of_mine[2] + of_mate[2])
    grad_hidden = jnp.sum(spread(by_task, "tensor", n_tensor), axis=0)
    grad_pre = grad_hidden * silu_slope(pre_act)
    grad_hyper_in = lax.dot_general(
        task_embed.astype(f32), grad_pre, outer_dims, precision=precise
    )

    adapter = lax.dot_general(
        low_rows.astype(f32), up_cat.astype(f32), inner_dims, precision=precise
    )
    values = (frozen_rows + adapter).astype(bf16)
    adapter_back = lax.dot_general(back_low, down_cat, inner_dims, preferred_element_type=f32)
    frozen_back = jnp.dot(cot_full, weight_t, preferred_element_type=f32)
    grad_tokens = (frozen_back + adapter_back).astype(bf16)
    return (values, grad_tokens, grad_head_a, grad_head_b, grad_hyper_in)


def solution(mesh):
    placed = (
        P("dp", "tensor"),
        P("tensor", "dp"),
        P("dp", None),
        P(),
        P(),
        P(None, "dp"),
        P("dp", "tensor"),
        P("dp", "tensor"),
        P(("dp", "tensor"), None),
    )
    return jax.shard_map(
        shards,
        mesh=mesh,
        in_specs=placed,
        out_specs=(
            P(("dp", "tensor"), None),
            P("dp", "tensor"),
            P("dp", "tensor"),
            P("dp", "tensor"),
            P(None, "dp"),
        ),
        check_vma=False,
    )
```

```python
import math

import jax
import jax.numpy as jnp
from jax import lax
from jax.sharding import PartitionSpec as P

D = 8192
KV = 512
R = 8
NTASK = 32
SEQS = 2
ADA = SEQS * R

precise = lax.Precision.HIGHEST
inner_dims = (((1,), (1,)), ((), ()))
outer_dims = (((0,), (0,)), ((), ()))
bf16 = jnp.bfloat16
f32 = jnp.float32

CORES = 2
Y_RUN = 4


def silu_slope(pre_act):
    sigma = jax.nn.sigmoid(pre_act)
    return sigma * (1.0 + pre_act * (1.0 - sigma))


def spread(block, axes, count, **kw):
    copies = jnp.broadcast_to(block[None], (count,) + block.shape)
    return lax.all_to_all(copies, axes, 0, 0, **kw)


def swapped(block, axis, distance):
    pairs = [(i, i ^ distance) for i in range(lax.axis_size(axis))]
    return lax.ppermute(block, axis, pairs)


def zero_after(value):
    first = value.reshape(-1)[0].astype(f32)
    return (jnp.floor(first) > first).astype(jnp.int32)


def parts_of(value):
    parts = []
    for _ in range(3):
        part = lax.reduce_precision(value, 8, 7)
        parts.append(part.astype(bf16))
        value = value - part
    return parts


def shards(
    tokens, value_weight, seq_lengths, task_ids, task_embed, hyper_in, head_a, head_b, cotangent
):
    n_dp = lax.axis_size("dp")
    n_chips = n_dp // CORES
    n_tensor = lax.axis_size("tensor")
    n_x = n_tensor // Y_RUN
    rows_total, width_own = tokens.shape
    rows_own = rows_total // n_tensor
    outputs_own = KV // n_tensor
    down_width = width_own * R
    up_width = outputs_own * R
    along_y = [[x * Y_RUN + y for y in range(Y_RUN)] for x in range(n_x)]
    along_x = [[x * Y_RUN + y for x in range(n_x)] for y in range(Y_RUN)]
    same_core = [[chip * CORES + core for chip in range(n_chips)] for core in range(CORES)]
    core = lax.axis_index("dp") % CORES
    place = lax.axis_index("tensor")

    pre_act = jnp.dot(task_embed, hyper_in, preferred_element_type=f32)
    hidden = jax.nn.silu(pre_act).astype(bf16)

    def chosen_by(which):
        ids = lax.dynamic_index_in_dim(
            task_ids.reshape(n_chips, CORES, SEQS), which, 1, keepdims=False
        ).reshape(n_chips * SEQS)
        hot = (ids[:, None] == jnp.arange(NTASK, dtype=jnp.int32)[None, :]).astype(bf16)
        return hot, jnp.dot(hot, hidden, preferred_element_type=f32).astype(bf16)

    def terms_of(pick):
        return jnp.concatenate(
            (
                jnp.dot(pick, head_a, preferred_element_type=f32),
                jnp.dot(pick, head_b, preferred_element_type=f32),
            ),
            axis=1,
        )

    hot_mate, pick_mate = chosen_by(1 - core)
    hot_mine, pick_mine = chosen_by(core)
    from_mate = swapped(terms_of(pick_mate).astype(bf16), "dp", 1)
    terms = (terms_of(pick_mine) + from_mate.astype(f32)).astype(bf16)
    term_width = down_width + up_width
    weight_own = value_weight.T.reshape(1, SEQS, -1)
    sent = jnp.concatenate(
        (
            terms.reshape(n_chips, SEQS, term_width),
            jnp.broadcast_to(weight_own, (n_chips,) + weight_own.shape[1:]),
        ),
        axis=2,
    )
    came = lax.all_to_all(sent, "dp", 0, 0, axis_index_groups=same_core)
    sums = jnp.sum(came[:, :, :term_width].astype(f32), axis=0)
    down_pick = (sums[:, :down_width] * (1.0 / math.sqrt(D))).astype(bf16)
    up_pick = (sums[:, down_width:] * (1.0 / math.sqrt(R))).astype(bf16)
    down_cat_t = (
        down_pick.reshape(SEQS, width_own, R).transpose(0, 2, 1).reshape(ADA, width_own)
    )
    up_pick_t = (
        up_pick.reshape(SEQS, outputs_own, R).transpose(0, 2, 1).reshape(ADA, outputs_own)
    )

    lengths = seq_lengths[0]
    finish = jnp.cumsum(lengths)
    anchor = finish - lengths
    places = jnp.arange(rows_total, dtype=jnp.int32)[None, :]
    inside = (places >= anchor[:SEQS, None]) & (places < finish[:SEQS, None])
    row_mask = jnp.repeat(inside.astype(f32), R, axis=0)

    low_part = (
        lax.dot_general(down_cat_t, tokens, inner_dims, preferred_element_type=f32) * row_mask
    ).astype(bf16)
    low_lines = ADA * rows_total // KV

    def as_lines(rows):
        return jnp.concatenate(
            [rows[:, i * KV : (i + 1) * KV] for i in range(rows_total // KV)], axis=0
        )

    def as_rows(lines):
        return jnp.concatenate(
            [lines[i * ADA : (i + 1) * ADA] for i in range(rows_total // KV)], axis=1
        )

    up_line = up_pick_t.reshape(-1, KV)
    block = jnp.concatenate((cotangent, as_lines(low_part), up_line), axis=0)
    from_y = spread(block, "tensor", Y_RUN, axis_index_groups=along_y)
    low_y = jnp.sum(from_y[:, rows_own : rows_own + low_lines].astype(f32), axis=0).astype(bf16)
    run_rows = Y_RUN * rows_own
    run = jnp.concatenate(
        (
            from_y[:, :rows_own].reshape(run_rows, KV),
            low_y,
            from_y[:, rows_own + low_lines :].reshape(-1, KV),
        ),
        axis=0,
    )
    from_x = spread(run, "tensor", n_x, axis_index_groups=along_x)
    cot_full = from_x[:, :run_rows].reshape(rows_total, KV)
    low_rank = as_rows(
        jnp.sum(from_x[:, run_rows : run_rows + low_lines].astype(f32), axis=0)
    )
    up_cat_t = (
        from_x[:, run_rows + low_lines :]
        .reshape(n_tensor, ADA, outputs_own)
        .transpose(1, 0, 2)
        .reshape(ADA, KV)
    )

    weight_mine = came[:, :, term_width:]
    weight_mate = swapped(weight_mine, "dp", 1)
    weight_mine = weight_mine.reshape(n_chips, KV // n_dp, width_own)
    weight_mate = weight_mate.reshape(n_chips, KV // n_dp, width_own)
    weight_t = jnp.stack(
        (
            jnp.where(core == 0, weight_mine, weight_mate),
            jnp.where(core == 0, weight_mate, weight_mine),
        ),
        axis=1,
    ).reshape(KV, width_own)
    weight_full = lax.optimization_barrier(weight_t.T)
    frozen = jnp.dot(tokens, weight_full, preferred_element_type=f32).astype(bf16)

    back_low = (
        lax.dot_general(up_cat_t, cot_full, inner_dims, preferred_element_type=f32) * row_mask
    ).astype(bf16)
    down_grad = jnp.dot(back_low, tokens, preferred_element_type=f32)
    down_seq = down_grad.reshape(SEQS, R, width_own).transpose(0, 2, 1).reshape(SEQS, down_width)
    low_parts = jnp.concatenate(parts_of(low_rank), axis=0)
    up_grad = jnp.sum(
        jnp.dot(low_parts, cot_full, preferred_element_type=f32).reshape(3, ADA, KV), axis=0
    )
    up_grad = lax.dynamic_slice_in_dim(up_grad, place * outputs_own, outputs_own, 1)
    up_seq = up_grad.reshape(SEQS, R, outputs_own).transpose(0, 2, 1).reshape(SEQS, up_width)
    own_grads = jnp.concatenate((down_seq, up_seq), axis=1).astype(bf16)
    grads_mine = spread(own_grads, "dp", n_chips, axis_index_groups=same_core)
    adapter_back = lax.dot_general(back_low, down_cat_t, outer_dims, preferred_element_type=f32)
    frozen_back = jnp.dot(cot_full, weight_t, preferred_element_type=f32)
    grad_tokens = (frozen_back + adapter_back).astype(bf16)
    frozen_x = frozen.reshape(n_x, Y_RUN * rows_own, KV)
    place_x = place // Y_RUN
    frozen_kept = lax.dynamic_index_in_dim(frozen_x, place_x, 0, keepdims=False)
    later = zero_after(grad_tokens[:1, :1])
    frozen_came = [
        swapped(
            lax.dynamic_index_in_dim(frozen_x, (place_x ^ step) + later, 0, keepdims=False),
            "tensor",
            step * Y_RUN,
        )
        for step in range(1, n_x)
    ]
    grads_mate = swapped(grads_mine, "dp", 1)

    down_scale = 1.0 / math.sqrt(D)
    up_scale = 1.0 / math.sqrt(R)

    def hidden_terms(grads, hot):
        rows = grads.reshape(n_chips * SEQS, -1)
        part = down_scale * lax.dot_general(
            rows[:, :down_width], head_a, inner_dims, preferred_element_type=f32
        ) + up_scale * lax.dot_general(
            rows[:, down_width:], head_b, inner_dims, preferred_element_type=f32
        )
        return lax.dot_general(hot.astype(f32), part, outer_dims, precision=precise)

    by_task = hidden_terms(grads_mine, hot_mine) + hidden_terms(grads_mate, hot_mate)
    hidden_x = jnp.sum(
        spread(by_task.reshape(1, -1), "tensor", n_x, axis_index_groups=along_x), axis=0
    )

    rows_x = frozen_kept.astype(f32)
    for other in frozen_came:
        rows_x = rows_x + other.astype(f32)
    last = jnp.concatenate(
        (
            rows_x.astype(bf16).reshape(Y_RUN, rows_own, KV),
            jnp.broadcast_to(
                jnp.concatenate(parts_of(hidden_x), axis=0).reshape(1, -1, KV),
                (Y_RUN, 3 * hidden_x.size // KV, KV),
            ),
        ),
        axis=1,
    )
    last = jnp.sum(
        lax.all_to_all(last, "tensor", 0, 0, axis_index_groups=along_y).astype(f32), axis=0
    )
    frozen_rows = last[:rows_own]
    grad_hidden = jnp.sum(last[rows_own:].reshape((3,) + by_task.shape), axis=0)

    last_zero = zero_after(hidden_x).astype(bf16)

    def head_grads(grads, pick):
        rows = grads.reshape(n_chips * SEQS, -1)
        pick = pick + last_zero
        return (
            lax.dot_general(pick, rows[:, :down_width], outer_dims, preferred_element_type=f32),
            lax.dot_general(pick, rows[:, down_width:], outer_dims, preferred_element_type=f32),
        )

    of_mine = head_grads(grads_mine, pick_mine)
    of_mate = head_grads(grads_mate, pick_mate)
    grad_head_a = down_scale * (of_mine[0] + of_mate[0])
    grad_head_b = up_scale * (of_mine[1] + of_mate[1])
    grad_pre = grad_hidden * silu_slope(pre_act)
    grad_hyper_in = lax.dot_general(
        task_embed.astype(f32), grad_pre, outer_dims, precision=precise
    )

    low_own = lax.dynamic_slice_in_dim(low_rank, place * rows_own, rows_own, 1)
    adapter = lax.dot_general(low_own, up_cat_t.astype(f32), outer_dims, precision=precise)
    values = (frozen_rows + adapter).astype(bf16)
    return (values, grad_tokens, grad_head_a, grad_head_b, grad_hyper_in)


def solution(mesh):
    placed = (
        P("dp", "tensor"),
        P("tensor", "dp"),
        P("dp", None),
        P(),
        P(),
        P(None, "dp"),
        P("dp", "tensor"),
        P("dp", "tensor"),
        P(("dp", "tensor"), None),
    )
    return jax.shard_map(
        shards,
        mesh=mesh,
        in_specs=placed,
        out_specs=(
            P(("dp", "tensor"), None),
            P("dp", "tensor"),
            P("dp", "tensor"),
            P("dp", "tensor"),
            P(None, "dp"),
        ),
        check_vma=False,
    )
```

```python
import math

import jax
import jax.numpy as jnp
from jax import lax
from jax.sharding import PartitionSpec as P

D = 8192
KV = 512
R = 8
NTASK = 32
SEQS = 2
ADA = SEQS * R

precise = lax.Precision.HIGHEST
inner_dims = (((1,), (1,)), ((), ()))
outer_dims = (((0,), (0,)), ((), ()))
bf16 = jnp.bfloat16
f32 = jnp.float32

CORES = 2
Y_RUN = 4


def silu_slope(pre_act):
    sigma = jax.nn.sigmoid(pre_act)
    return sigma * (1.0 + pre_act * (1.0 - sigma))


def spread(block, axes, count, **kw):
    copies = jnp.broadcast_to(block[None], (count,) + block.shape)
    return lax.all_to_all(copies, axes, 0, 0, **kw)


def swapped(block, axis, distance):
    pairs = [(i, i ^ distance) for i in range(lax.axis_size(axis))]
    return lax.ppermute(block, axis, pairs)


def zero_after(value):
    first = value.reshape(-1)[0].astype(f32)
    return (jnp.floor(first) > first).astype(jnp.int32)


def parts_of(value):
    parts = []
    for _ in range(3):
        part = lax.reduce_precision(value, 8, 7)
        parts.append(part.astype(bf16))
        value = value - part
    return parts


def gathered(block, part, count, stride, later=0):
    every = jnp.zeros((count,) + block.shape, block.dtype)
    every = lax.dynamic_update_index_in_dim(every, block, part + later, 0)
    for step in range(1, count):
        other = swapped(block, "tensor", step * stride)
        every = lax.dynamic_update_index_in_dim(every, other, (part ^ step) + later, 0)
    return every.reshape((count * block.shape[0],) + block.shape[1:])


def shards(
    tokens, value_weight, seq_lengths, task_ids, task_embed, hyper_in, head_a, head_b, cotangent
):
    n_dp = lax.axis_size("dp")
    n_chips = n_dp // CORES
    n_tensor = lax.axis_size("tensor")
    n_x = n_tensor // Y_RUN
    rows_total, width_own = tokens.shape
    rows_own = rows_total // n_tensor
    outputs_own = KV // n_tensor
    down_width = width_own * R
    up_width = outputs_own * R
    along_y = [[x * Y_RUN + y for y in range(Y_RUN)] for x in range(n_x)]
    along_x = [[x * Y_RUN + y for x in range(n_x)] for y in range(Y_RUN)]
    same_core = [[chip * CORES + core for chip in range(n_chips)] for core in range(CORES)]
    core = lax.axis_index("dp") % CORES
    place = lax.axis_index("tensor")

    pre_act = jnp.dot(task_embed, hyper_in, preferred_element_type=f32)
    hidden = jax.nn.silu(pre_act).astype(bf16)

    def chosen_by(which):
        ids = lax.dynamic_index_in_dim(
            task_ids.reshape(n_chips, CORES, SEQS), which, 1, keepdims=False
        ).reshape(n_chips * SEQS)
        hot = (ids[:, None] == jnp.arange(NTASK, dtype=jnp.int32)[None, :]).astype(bf16)
        return hot, jnp.dot(hot, hidden, preferred_element_type=f32).astype(bf16)

    def terms_of(pick):
        return jnp.concatenate(
            (
                jnp.dot(pick, head_a, preferred_element_type=f32),
                jnp.dot(pick, head_b, preferred_element_type=f32),
            ),
            axis=1,
        )

    hot_mate, pick_mate = chosen_by(1 - core)
    hot_mine, pick_mine = chosen_by(core)
    from_mate = swapped(terms_of(pick_mate).astype(bf16), "dp", 1)
    terms = (terms_of(pick_mine) + from_mate.astype(f32)).astype(bf16)
    term_width = down_width + up_width
    weight_own = value_weight.T.reshape(1, SEQS, -1)
    sent = jnp.concatenate(
        (
            terms.reshape(n_chips, SEQS, term_width),
            jnp.broadcast_to(weight_own, (n_chips,) + weight_own.shape[1:]),
        ),
        axis=2,
    )
    came = lax.all_to_all(sent, "dp", 0, 0, axis_index_groups=same_core)
    sums = jnp.sum(came[:, :, :term_width].astype(f32), axis=0)
    down_pick = (sums[:, :down_width] * (1.0 / math.sqrt(D))).astype(bf16)
    up_pick = (sums[:, down_width:] * (1.0 / math.sqrt(R))).astype(bf16)
    down_cat_t = (
        down_pick.reshape(SEQS, width_own, R).transpose(0, 2, 1).reshape(ADA, width_own)
    )
    up_pick_t = (
        up_pick.reshape(SEQS, outputs_own, R).transpose(0, 2, 1).reshape(ADA, outputs_own)
    )

    cot_own = cotangent + zero_after(sent[:1, :1, :1]).astype(bf16)
    cot_run = gathered(cot_own, place % Y_RUN, Y_RUN, 1)
    lengths = seq_lengths[0]
    finish = jnp.cumsum(lengths)
    anchor = finish - lengths
    places = jnp.arange(rows_total, dtype=jnp.int32)[None, :]
    inside = (places >= anchor[:SEQS, None]) & (places < finish[:SEQS, None])
    row_mask = jnp.repeat(inside.astype(f32), R, axis=0)

    low_part = (
        lax.dot_general(down_cat_t, tokens, inner_dims, preferred_element_type=f32) * row_mask
    ).astype(bf16)
    cot_full = gathered(
        cot_run, place // Y_RUN, n_x, Y_RUN, zero_after(jnp.max(low_part, axis=0))
    )
    low_came = spread(jnp.concatenate((low_part, up_pick_t), axis=1), "tensor", n_tensor)
    low_rank = jnp.sum(low_came[:, :, :rows_total].astype(f32), axis=0)
    up_cat_t = low_came[:, :, rows_total:].transpose(1, 0, 2).reshape(ADA, KV)

    weight_mine = came[:, :, term_width:]
    weight_mate = swapped(weight_mine, "dp", 1)
    weight_mine = weight_mine.reshape(n_chips, KV // n_dp, width_own)
    weight_mate = weight_mate.reshape(n_chips, KV // n_dp, width_own)
    weight_t = jnp.stack(
        (
            jnp.where(core == 0, weight_mine, weight_mate),
            jnp.where(core == 0, weight_mate, weight_mine),
        ),
        axis=1,
    ).reshape(KV, width_own)
    weight_full = lax.optimization_barrier(weight_t.T)
    frozen = jnp.dot(tokens, weight_full, preferred_element_type=f32).astype(bf16)

    back_low = (
        lax.dot_general(up_cat_t, cot_full, inner_dims, preferred_element_type=f32) * row_mask
    ).astype(bf16)
    down_grad = jnp.dot(back_low, tokens, preferred_element_type=f32)
    down_seq = down_grad.reshape(SEQS, R, width_own).transpose(0, 2, 1).reshape(SEQS, down_width)
    low_parts = jnp.concatenate(parts_of(low_rank), axis=0)
    up_grad = jnp.sum(
        jnp.dot(low_parts, cot_full, preferred_element_type=f32).reshape(3, ADA, KV), axis=0
    )
    up_grad = lax.dynamic_slice_in_dim(up_grad, place * outputs_own, outputs_own, 1)
    up_seq = up_grad.reshape(SEQS, R, outputs_own).transpose(0, 2, 1).reshape(SEQS, up_width)
    own_grads = jnp.concatenate((down_seq, up_seq), axis=1).astype(bf16)
    grads_mine = spread(own_grads, "dp", n_chips, axis_index_groups=same_core)
    adapter_back = lax.dot_general(back_low, down_cat_t, outer_dims, preferred_element_type=f32)
    frozen_back = jnp.dot(cot_full, weight_t, preferred_element_type=f32)
    grad_tokens = (frozen_back + adapter_back).astype(bf16)
    frozen_x = frozen.reshape(n_x, Y_RUN * rows_own, KV)
    place_x = place // Y_RUN
    frozen_kept = lax.dynamic_index_in_dim(frozen_x, place_x, 0, keepdims=False)
    later = zero_after(grad_tokens[:1, :1])
    frozen_came = [
        swapped(
            lax.dynamic_index_in_dim(frozen_x, (place_x ^ step) + later, 0, keepdims=False),
            "tensor",
            step * Y_RUN,
        )
        for step in range(1, n_x)
    ]
    grads_mate = swapped(grads_mine, "dp", 1)

    down_scale = 1.0 / math.sqrt(D)
    up_scale = 1.0 / math.sqrt(R)

    def hidden_terms(grads, hot):
        rows = grads.reshape(n_chips * SEQS, -1)
        part = down_scale * lax.dot_general(
            rows[:, :down_width], head_a, inner_dims, preferred_element_type=f32
        ) + up_scale * lax.dot_general(
            rows[:, down_width:], head_b, inner_dims, preferred_element_type=f32
        )
        return lax.dot_general(hot.astype(f32), part, outer_dims, precision=precise)

    by_task = hidden_terms(grads_mine, hot_mine) + hidden_terms(grads_mate, hot_mate)
    hidden_x = jnp.sum(
        spread(by_task.reshape(1, -1), "tensor", n_x, axis_index_groups=along_x), axis=0
    )

    rows_x = frozen_kept.astype(f32)
    for other in frozen_came:
        rows_x = rows_x + other.astype(f32)
    last = jnp.concatenate(
        (
            rows_x.astype(bf16).reshape(Y_RUN, rows_own, KV),
            jnp.broadcast_to(
                jnp.concatenate(parts_of(hidden_x), axis=0).reshape(1, -1, KV),
                (Y_RUN, 3 * hidden_x.size // KV, KV),
            ),
        ),
        axis=1,
    )
    last = jnp.sum(
        lax.all_to_all(last, "tensor", 0, 0, axis_index_groups=along_y).astype(f32), axis=0
    )
    frozen_rows = last[:rows_own]
    grad_hidden = jnp.sum(last[rows_own:].reshape((3,) + by_task.shape), axis=0)

    last_zero = zero_after(hidden_x).astype(bf16)

    def head_grads(grads, pick):
        rows = grads.reshape(n_chips * SEQS, -1)
        pick = pick + last_zero
        return (
            lax.dot_general(pick, rows[:, :down_width], outer_dims, preferred_element_type=f32),
            lax.dot_general(pick, rows[:, down_width:], outer_dims, preferred_element_type=f32),
        )

    of_mine = head_grads(grads_mine, pick_mine)
    of_mate = head_grads(grads_mate, pick_mate)
    grad_head_a = down_scale * (of_mine[0] + of_mate[0])
    grad_head_b = up_scale * (of_mine[1] + of_mate[1])
    grad_pre = grad_hidden * silu_slope(pre_act)
    grad_hyper_in = lax.dot_general(
        task_embed.astype(f32), grad_pre, outer_dims, precision=precise
    )

    low_own = lax.dynamic_slice_in_dim(low_rank, place * rows_own, rows_own, 1)
    adapter = lax.dot_general(low_own, up_cat_t.astype(f32), outer_dims, precision=precise)
    values = (frozen_rows + adapter).astype(bf16)
    return (values, grad_tokens, grad_head_a, grad_head_b, grad_hyper_in)


def solution(mesh):
    placed = (
        P("dp", "tensor"),
        P("tensor", "dp"),
        P("dp", None),
        P(),
        P(),
        P(None, "dp"),
        P("dp", "tensor"),
        P("dp", "tensor"),
        P(("dp", "tensor"), None),
    )
    return jax.shard_map(
        shards,
        mesh=mesh,
        in_specs=placed,
        out_specs=(
            P(("dp", "tensor"), None),
            P("dp", "tensor"),
            P("dp", "tensor"),
            P("dp", "tensor"),
            P(None, "dp"),
        ),
        check_vma=False,
    )
```

```python
import math

import jax
import jax.numpy as jnp
from jax import lax
from jax.sharding import PartitionSpec as P

D = 8192
KV = 512
R = 8
NTASK = 32
SEQS = 2
ADA = SEQS * R

precise = lax.Precision.HIGHEST
inner_dims = (((1,), (1,)), ((), ()))
outer_dims = (((0,), (0,)), ((), ()))
bf16 = jnp.bfloat16
f32 = jnp.float32

CORES = 2
Y_RUN = 4


def silu_slope(pre_act):
    sigma = jax.nn.sigmoid(pre_act)
    return sigma * (1.0 + pre_act * (1.0 - sigma))


def spread(block, axes, count, **kw):
    copies = jnp.broadcast_to(block[None], (count,) + block.shape)
    return lax.all_to_all(copies, axes, 0, 0, **kw)


def swapped(block, axis, distance):
    pairs = [(i, i ^ distance) for i in range(lax.axis_size(axis))]
    return lax.ppermute(block, axis, pairs)


def zero_after(value):
    first = value.reshape(-1)[0].astype(f32)
    return (jnp.floor(first) > first).astype(jnp.int32)


def parts_of(value):
    parts = []
    for _ in range(3):
        part = lax.reduce_precision(value, 8, 7)
        parts.append(part.astype(bf16))
        value = value - part
    return parts


def gathered(block, part, count, stride):
    every = jnp.zeros((count,) + block.shape, block.dtype)
    every = lax.dynamic_update_index_in_dim(every, block, part, 0)
    for step in range(1, count):
        other = swapped(block, "tensor", step * stride)
        every = lax.dynamic_update_index_in_dim(every, other, part ^ step, 0)
    return every.reshape((count * block.shape[0],) + block.shape[1:])


def shards(
    tokens, value_weight, seq_lengths, task_ids, task_embed, hyper_in, head_a, head_b, cotangent
):
    n_dp = lax.axis_size("dp")
    n_chips = n_dp // CORES
    n_tensor = lax.axis_size("tensor")
    n_x = n_tensor // Y_RUN
    rows_total, width_own = tokens.shape
    rows_own = rows_total // n_tensor
    outputs_own = KV // n_tensor
    down_width = width_own * R
    up_width = outputs_own * R
    along_y = [[x * Y_RUN + y for y in range(Y_RUN)] for x in range(n_x)]
    along_x = [[x * Y_RUN + y for x in range(n_x)] for y in range(Y_RUN)]
    same_core = [[chip * CORES + core for chip in range(n_chips)] for core in range(CORES)]
    core = lax.axis_index("dp") % CORES
    place = lax.axis_index("tensor")

    cot_run = spread(cotangent, "tensor", Y_RUN, axis_index_groups=along_y).reshape(-1, KV)

    pre_act = jnp.dot(task_embed, hyper_in, preferred_element_type=f32)
    hidden = jax.nn.silu(pre_act).astype(bf16)

    def chosen_by(which):
        ids = lax.dynamic_index_in_dim(
            task_ids.reshape(n_chips, CORES, SEQS), which, 1, keepdims=False
        ).reshape(n_chips * SEQS)
        hot = (ids[:, None] == jnp.arange(NTASK, dtype=jnp.int32)[None, :]).astype(bf16)
        return hot, jnp.dot(hot, hidden, preferred_element_type=f32).astype(bf16)

    heads = jnp.concatenate((head_a, head_b), axis=1)

    def terms_of(pick):
        return jnp.dot(pick, heads, preferred_element_type=f32)

    hot_mate, pick_mate = chosen_by(1 - core)
    hot_mine, pick_mine = chosen_by(core)
    from_mate = swapped(terms_of(pick_mate).astype(bf16), "dp", 1)
    terms = (terms_of(pick_mine) + from_mate.astype(f32)).astype(bf16)
    term_width = down_width + up_width
    weight_own = value_weight.T.reshape(1, SEQS, -1)
    sent = jnp.concatenate(
        (
            terms.reshape(n_chips, SEQS, term_width),
            jnp.broadcast_to(weight_own, (n_chips,) + weight_own.shape[1:]),
        ),
        axis=2,
    )
    came = lax.all_to_all(sent, "dp", 0, 0, axis_index_groups=same_core)
    sums = jnp.sum(came[:, :, :term_width].astype(f32), axis=0)
    down_pick = (sums[:, :down_width] * (1.0 / math.sqrt(D))).astype(bf16)
    up_pick = (sums[:, down_width:] * (1.0 / math.sqrt(R))).astype(bf16)
    down_cat = down_pick.reshape(SEQS, width_own, R).transpose(1, 0, 2).reshape(width_own, ADA)

    place_x = place // Y_RUN
    cot_full = gathered(cot_run, place_x, n_x, Y_RUN)

    first, second = seq_lengths[0, 0], seq_lengths[0, 1]
    places = jnp.arange(rows_total, dtype=jnp.int32)[:, None]
    in_second = (places >= first) & (places < first + second)
    in_first = jnp.broadcast_to(places < first, (rows_total, R))
    col_mask = jnp.concatenate(
        (in_first, jnp.broadcast_to(in_second, (rows_total, R))), axis=1
    ).astype(f32)

    low_part = (jnp.dot(tokens, down_cat, preferred_element_type=f32) * col_mask).astype(bf16)
    up_part = lax.dot_general(cot_full, low_part, outer_dims, preferred_element_type=f32).astype(
        bf16
    )
    low_lines = rows_own * ADA // KV
    up_lines = outputs_own * ADA // KV
    pick_lines = SEQS * up_width // KV
    block = jnp.concatenate(
        (
            low_part.reshape(n_tensor, low_lines, KV),
            up_part.reshape(n_tensor, up_lines, KV),
            jnp.broadcast_to(up_pick.reshape(1, pick_lines, KV), (n_tensor, pick_lines, KV)),
        ),
        axis=1,
    )
    summed = low_lines + up_lines
    low_came = lax.all_to_all(block, "tensor", 0, 0)
    whole = jnp.sum(low_came[:, :summed].astype(f32), axis=0)
    low_rows = whole[:low_lines].reshape(rows_own, ADA)
    up_grad = whole[low_lines:].reshape(outputs_own, ADA)
    up_cat = (
        low_came[:, summed:]
        .reshape(n_tensor, SEQS, outputs_own, R)
        .transpose(0, 2, 1, 3)
        .reshape(KV, ADA)
    )

    weight_mine = came[:, :, term_width:]
    weight_mate = swapped(weight_mine, "dp", 1)
    weight_mine = weight_mine.reshape(n_chips, KV // n_dp, width_own)
    weight_mate = weight_mate.reshape(n_chips, KV // n_dp, width_own)
    weight_t = jnp.stack(
        (
            jnp.where(core == 0, weight_mine, weight_mate),
            jnp.where(core == 0, weight_mate, weight_mine),
        ),
        axis=1,
    ).reshape(KV, width_own)
    frozen_t = lax.dot_general(
        weight_t, tokens, inner_dims, preferred_element_type=f32
    ).astype(bf16)

    down_scale = 1.0 / math.sqrt(D)
    up_scale = 1.0 / math.sqrt(R)
    back_low = (jnp.dot(cot_full, up_cat, preferred_element_type=f32) * col_mask).astype(bf16)
    down_grad = down_scale * lax.dot_general(
        tokens, back_low, outer_dims, preferred_element_type=f32
    )
    up_grad = up_scale * up_grad
    down_seq = down_grad.reshape(width_own, SEQS, R).transpose(1, 0, 2).reshape(SEQS, down_width)
    up_seq = up_grad.reshape(outputs_own, SEQS, R).transpose(1, 0, 2).reshape(SEQS, up_width)
    own_grads = jnp.concatenate((down_seq, up_seq), axis=1).astype(bf16)
    grads_mine = spread(own_grads, "dp", n_chips, axis_index_groups=same_core)

    adapter_back = lax.dot_general(back_low, down_cat, inner_dims, preferred_element_type=f32)
    frozen_back = jnp.dot(cot_full, weight_t, preferred_element_type=f32)
    grad_tokens = (frozen_back + adapter_back).astype(bf16)
    run_rows = Y_RUN * rows_own

    def run_of(x):
        return lax.dynamic_slice_in_dim(frozen_t, x * run_rows, run_rows, 1)

    frozen_kept = run_of(place_x)
    frozen_came = [
        swapped(run_of(place_x ^ step), "tensor", step * Y_RUN)
        for step in range(1, n_x)
    ]
    grads_mate = swapped(grads_mine, "dp", 1)

    def hidden_terms(grads, hot):
        part = lax.dot_general(
            grads.reshape(n_chips * SEQS, -1), heads, inner_dims, preferred_element_type=f32
        )
        return lax.dot_general(hot.astype(f32), part, outer_dims, precision=precise)

    by_task = hidden_terms(grads_mine, hot_mine) + hidden_terms(grads_mate, hot_mate)
    hidden_x = jnp.sum(
        spread(by_task.reshape(1, -1), "tensor", n_x, axis_index_groups=along_x), axis=0
    )

    rows_x = frozen_kept.astype(f32)
    for other in frozen_came:
        rows_x = rows_x + other.astype(f32)
    last = jnp.concatenate(
        (
            rows_x.astype(bf16).T.reshape(Y_RUN, rows_own, KV),
            jnp.broadcast_to(
                jnp.concatenate(parts_of(hidden_x), axis=0).reshape(1, -1, KV),
                (Y_RUN, 3 * hidden_x.size // KV, KV),
            ),
        ),
        axis=1,
    )
    last = jnp.sum(
        lax.all_to_all(last, "tensor", 0, 0, axis_index_groups=along_y).astype(f32), axis=0
    )
    frozen_rows = last[:rows_own]
    grad_hidden = jnp.sum(last[rows_own:].reshape((3,) + by_task.shape), axis=0)

    last_zero = zero_after(hidden_x).astype(bf16)

    def head_grads(grads, pick):
        return lax.dot_general(
            pick + last_zero,
            grads.reshape(n_chips * SEQS, -1),
            outer_dims,
            preferred_element_type=f32,
        )

    grad_heads = head_grads(grads_mine, pick_mine) + head_grads(grads_mate, pick_mate)
    grad_head_a = grad_heads[:, :down_width]
    grad_head_b = grad_heads[:, down_width:]
    grad_pre = grad_hidden * silu_slope(pre_act)
    grad_hyper_in = lax.dot_general(
        task_embed.astype(f32), grad_pre, outer_dims, precision=precise
    )

    adapter = lax.dot_general(
        low_rows.astype(f32), up_cat.astype(f32), inner_dims, precision=precise
    )
    values = (frozen_rows + adapter).astype(bf16)
    return (values, grad_tokens, grad_head_a, grad_head_b, grad_hyper_in)


def solution(mesh):
    placed = (
        P("dp", "tensor"),
        P("tensor", "dp"),
        P("dp", None),
        P(),
        P(),
        P(None, "dp"),
        P("dp", "tensor"),
        P("dp", "tensor"),
        P(("dp", "tensor"), None),
    )
    return jax.shard_map(
        shards,
        mesh=mesh,
        in_specs=placed,
        out_specs=(
            P(("dp", "tensor"), None),
            P("dp", "tensor"),
            P("dp", "tensor"),
            P("dp", "tensor"),
            P(None, "dp"),
        ),
        check_vma=False,
    )
```

```python
import math

import jax
import jax.numpy as jnp
from jax import lax
from jax.sharding import PartitionSpec as P

D = 8192
KV = 512
R = 8
NTASK = 32
SEQS = 2
ADA = SEQS * R

precise = lax.Precision.HIGHEST
inner_dims = (((1,), (1,)), ((), ()))
outer_dims = (((0,), (0,)), ((), ()))
bf16 = jnp.bfloat16
f32 = jnp.float32

CORES = 2
Y_RUN = 4


def silu_slope(pre_act):
    sigma = jax.nn.sigmoid(pre_act)
    return sigma * (1.0 + pre_act * (1.0 - sigma))


def spread(block, axes, count, **kw):
    copies = jnp.broadcast_to(block[None], (count,) + block.shape)
    return lax.all_to_all(copies, axes, 0, 0, **kw)


def swapped(block, axis, distance):
    pairs = [(i, i ^ distance) for i in range(lax.axis_size(axis))]
    return lax.ppermute(block, axis, pairs)


def zero_after(value):
    first = value.reshape(-1)[0].astype(f32)
    return (jnp.floor(first) > first).astype(jnp.int32)


def parts_of(value):
    parts = []
    for _ in range(3):
        part = lax.reduce_precision(value, 8, 7)
        parts.append(part.astype(bf16))
        value = value - part
    return parts


def gathered(block, part, count, stride):
    every = jnp.zeros((count,) + block.shape, block.dtype)
    every = lax.dynamic_update_index_in_dim(every, block, part, 0)
    for step in range(1, count):
        other = swapped(block, "tensor", step * stride)
        every = lax.dynamic_update_index_in_dim(every, other, part ^ step, 0)
    return every.reshape((count * block.shape[0],) + block.shape[1:])


def shards(
    tokens, value_weight, seq_lengths, task_ids, task_embed, hyper_in, head_a, head_b, cotangent
):
    n_dp = lax.axis_size("dp")
    n_chips = n_dp // CORES
    n_tensor = lax.axis_size("tensor")
    n_x = n_tensor // Y_RUN
    rows_total, width_own = tokens.shape
    rows_own = rows_total // n_tensor
    outputs_own = KV // n_tensor
    down_width = width_own * R
    up_width = outputs_own * R
    along_y = [[x * Y_RUN + y for y in range(Y_RUN)] for x in range(n_x)]
    along_x = [[x * Y_RUN + y for x in range(n_x)] for y in range(Y_RUN)]
    same_core = [[chip * CORES + core for chip in range(n_chips)] for core in range(CORES)]
    core = lax.axis_index("dp") % CORES
    place = lax.axis_index("tensor")

    cot_run = spread(cotangent, "tensor", Y_RUN, axis_index_groups=along_y).reshape(-1, KV)

    pre_act = jnp.dot(task_embed, hyper_in, preferred_element_type=f32)
    hidden = jax.nn.silu(pre_act).astype(bf16)

    def chosen_by(which):
        ids = lax.dynamic_index_in_dim(
            task_ids.reshape(n_chips, CORES, SEQS), which, 1, keepdims=False
        ).reshape(n_chips * SEQS)
        hot = (ids[:, None] == jnp.arange(NTASK, dtype=jnp.int32)[None, :]).astype(bf16)
        return hot, jnp.dot(hot, hidden, preferred_element_type=f32).astype(bf16)

    heads = jnp.concatenate((head_a, head_b), axis=1)

    def terms_of(pick):
        return jnp.dot(pick, heads, preferred_element_type=f32)

    hot_mate, pick_mate = chosen_by(1 - core)
    hot_mine, pick_mine = chosen_by(core)
    from_mate = swapped(terms_of(pick_mate).astype(bf16), "dp", 1)
    run_zero = zero_after(cot_run).astype(bf16)
    terms = (terms_of(pick_mine + run_zero) + from_mate.astype(f32)).astype(bf16)
    term_width = down_width + up_width
    weight_own = value_weight.T.reshape(1, SEQS, -1)
    sent = jnp.concatenate(
        (
            terms.reshape(n_chips, SEQS, term_width),
            jnp.broadcast_to(weight_own, (n_chips,) + weight_own.shape[1:]),
        ),
        axis=2,
    )
    came = lax.all_to_all(sent, "dp", 0, 0, axis_index_groups=same_core)
    sums = jnp.sum(came[:, :, :term_width].astype(f32), axis=0)
    down_pick = (sums[:, :down_width] * (1.0 / math.sqrt(D))).astype(bf16)
    up_pick = (sums[:, down_width:] * (1.0 / math.sqrt(R))).astype(bf16)
    down_cat = down_pick.reshape(SEQS, width_own, R).transpose(1, 0, 2).reshape(width_own, ADA)

    place_x = place // Y_RUN
    cot_full = gathered(cot_run, place_x, n_x, Y_RUN)

    first, second = seq_lengths[0, 0], seq_lengths[0, 1]
    places = jnp.arange(rows_total, dtype=jnp.int32)[:, None]
    in_second = (places >= first) & (places < first + second)
    in_first = jnp.broadcast_to(places < first, (rows_total, R))
    col_mask = jnp.concatenate(
        (in_first, jnp.broadcast_to(in_second, (rows_total, R))), axis=1
    ).astype(f32)

    low_part = (jnp.dot(tokens, down_cat, preferred_element_type=f32) * col_mask).astype(bf16)
    up_part = lax.dot_general(cot_full, low_part, outer_dims, preferred_element_type=f32).astype(
        bf16
    )
    low_lines = rows_own * ADA // KV
    up_lines = outputs_own * ADA // KV
    pick_lines = SEQS * up_width // KV
    block = jnp.concatenate(
        (
            low_part.reshape(n_tensor, low_lines, KV),
            up_part.reshape(n_tensor, up_lines, KV),
            jnp.broadcast_to(up_pick.reshape(1, pick_lines, KV), (n_tensor, pick_lines, KV)),
        ),
        axis=1,
    )
    summed = low_lines + up_lines
    low_came = lax.all_to_all(block, "tensor", 0, 0)

    weight_mine = came[:, :, term_width:]
    weight_mate = swapped(weight_mine, "dp", 1)
    weight_mine = weight_mine.reshape(n_chips, KV // n_dp, width_own)
    weight_mate = weight_mate.reshape(n_chips, KV // n_dp, width_own)
    weight_t = jnp.stack(
        (
            jnp.where(core == 0, weight_mine, weight_mate),
            jnp.where(core == 0, weight_mate, weight_mine),
        ),
        axis=1,
    ).reshape(KV, width_own)
    frozen_t = lax.dot_general(
        weight_t, tokens, inner_dims, preferred_element_type=f32
    ).astype(bf16)

    low_came = low_came + zero_after(frozen_t).astype(bf16)
    whole = jnp.sum(low_came[:, :summed].astype(f32), axis=0)
    low_rows = whole[:low_lines].reshape(rows_own, ADA)
    up_grad = whole[low_lines:].reshape(outputs_own, ADA)
    up_cat = (
        low_came[:, summed:]
        .reshape(n_tensor, SEQS, outputs_own, R)
        .transpose(0, 2, 1, 3)
        .reshape(KV, ADA)
    )

    down_scale = 1.0 / math.sqrt(D)
    up_scale = 1.0 / math.sqrt(R)
    back_low = (jnp.dot(cot_full, up_cat, preferred_element_type=f32) * col_mask).astype(bf16)
    down_grad = down_scale * lax.dot_general(
        tokens, back_low, outer_dims, preferred_element_type=f32
    )
    up_grad = up_scale * up_grad
    down_seq = down_grad.reshape(width_own, SEQS, R).transpose(1, 0, 2).reshape(SEQS, down_width)
    up_seq = up_grad.reshape(outputs_own, SEQS, R).transpose(1, 0, 2).reshape(SEQS, up_width)
    own_grads = jnp.concatenate((down_seq, up_seq), axis=1).astype(bf16)
    grads_mine = spread(own_grads, "dp", n_chips, axis_index_groups=same_core)

    run_rows = Y_RUN * rows_own

    def run_of(x):
        return lax.dynamic_slice_in_dim(frozen_t, x * run_rows, run_rows, 1)

    frozen_kept = run_of(place_x)
    frozen_came = [
        swapped(run_of(place_x ^ step), "tensor", step * Y_RUN)
        for step in range(1, n_x)
    ]
    grads_mate = swapped(grads_mine, "dp", 1)

    def hidden_terms(grads, hot):
        part = lax.dot_general(
            grads.reshape(n_chips * SEQS, -1), heads, inner_dims, preferred_element_type=f32
        )
        return lax.dot_general(hot.astype(f32), part, outer_dims, precision=precise)

    by_task = hidden_terms(grads_mine, hot_mine) + hidden_terms(grads_mate, hot_mate)
    hidden_x = jnp.sum(
        spread(by_task.reshape(1, -1), "tensor", n_x, axis_index_groups=along_x), axis=0
    )

    rows_x = frozen_kept.astype(f32)
    for other in frozen_came:
        rows_x = rows_x + other.astype(f32)
    last = jnp.concatenate(
        (
            rows_x.astype(bf16).T.reshape(Y_RUN, rows_own, KV),
            jnp.broadcast_to(
                jnp.concatenate(parts_of(hidden_x), axis=0).reshape(1, -1, KV),
                (Y_RUN, 3 * hidden_x.size // KV, KV),
            ),
        ),
        axis=1,
    )
    last = jnp.sum(
        lax.all_to_all(last, "tensor", 0, 0, axis_index_groups=along_y).astype(f32), axis=0
    )
    frozen_rows = last[:rows_own]
    grad_hidden = jnp.sum(last[rows_own:].reshape((3,) + by_task.shape), axis=0)

    last_zero = zero_after(hidden_x).astype(bf16)

    adapter_back = lax.dot_general(back_low, down_cat, inner_dims, preferred_element_type=f32)
    frozen_back = jnp.dot(cot_full, weight_t, preferred_element_type=f32)
    grad_tokens = (frozen_back + last_zero.astype(f32) + adapter_back).astype(bf16)

    def head_grads(grads, pick):
        return lax.dot_general(
            pick + last_zero,
            grads.reshape(n_chips * SEQS, -1),
            outer_dims,
            preferred_element_type=f32,
        )

    grad_heads = head_grads(grads_mine, pick_mine) + head_grads(grads_mate, pick_mate)
    grad_head_a = grad_heads[:, :down_width]
    grad_head_b = grad_heads[:, down_width:]
    grad_pre = grad_hidden * silu_slope(pre_act)
    grad_hyper_in = lax.dot_general(
        task_embed.astype(f32), grad_pre, outer_dims, precision=precise
    )

    adapter = lax.dot_general(
        low_rows.astype(f32), up_cat.astype(f32), inner_dims, precision=precise
    )
    values = (frozen_rows + adapter).astype(bf16)
    return (values, grad_tokens, grad_head_a, grad_head_b, grad_hyper_in)


def solution(mesh):
    placed = (
        P("dp", "tensor"),
        P("tensor", "dp"),
        P("dp", None),
        P(),
        P(),
        P(None, "dp"),
        P("dp", "tensor"),
        P("dp", "tensor"),
        P(("dp", "tensor"), None),
    )
    return jax.shard_map(
        shards,
        mesh=mesh,
        in_specs=placed,
        out_specs=(
            P(("dp", "tensor"), None),
            P("dp", "tensor"),
            P("dp", "tensor"),
            P("dp", "tensor"),
            P(None, "dp"),
        ),
        check_vma=False,
    )
```

```python
import math

import jax
import jax.numpy as jnp
from jax import lax
from jax.sharding import PartitionSpec as P

D = 8192
KV = 512
R = 8
NTASK = 32
SEQS = 2
ADA = SEQS * R

precise = lax.Precision.HIGHEST
inner_dims = (((1,), (1,)), ((), ()))
outer_dims = (((0,), (0,)), ((), ()))
bf16 = jnp.bfloat16
f32 = jnp.float32

CORES = 2
Y_RUN = 4


def silu_slope(pre_act):
    sigma = jax.nn.sigmoid(pre_act)
    return sigma * (1.0 + pre_act * (1.0 - sigma))


def spread(block, axes, count, **kw):
    copies = jnp.broadcast_to(block[None], (count,) + block.shape)
    return lax.all_to_all(copies, axes, 0, 0, **kw)


def swapped(block, axis, distance):
    pairs = [(i, i ^ distance) for i in range(lax.axis_size(axis))]
    return lax.ppermute(block, axis, pairs)


def zero_after(value):
    first = value.reshape(-1)[0].astype(f32)
    return (jnp.floor(first) > first).astype(jnp.int32)


def parts_of(value):
    parts = []
    for _ in range(3):
        part = lax.reduce_precision(value, 8, 7)
        parts.append(part.astype(bf16))
        value = value - part
    return parts


def gathered(block, part, count, stride):
    every = jnp.zeros((count,) + block.shape, block.dtype)
    every = lax.dynamic_update_index_in_dim(every, block, part, 0)
    for step in range(1, count):
        other = swapped(block, "tensor", step * stride)
        every = lax.dynamic_update_index_in_dim(every, other, part ^ step, 0)
    return every.reshape((count * block.shape[0],) + block.shape[1:])


def shards(
    tokens, value_weight, seq_lengths, task_ids, task_embed, hyper_in, head_a, head_b, cotangent
):
    n_dp = lax.axis_size("dp")
    n_chips = n_dp // CORES
    n_tensor = lax.axis_size("tensor")
    n_x = n_tensor // Y_RUN
    rows_total, width_own = tokens.shape
    rows_own = rows_total // n_tensor
    outputs_own = KV // n_tensor
    down_width = width_own * R
    up_width = outputs_own * R
    along_y = [[x * Y_RUN + y for y in range(Y_RUN)] for x in range(n_x)]
    along_x = [[x * Y_RUN + y for x in range(n_x)] for y in range(Y_RUN)]
    same_core = [[chip * CORES + core for chip in range(n_chips)] for core in range(CORES)]
    core = lax.axis_index("dp") % CORES
    place = lax.axis_index("tensor")

    cot_run = spread(cotangent, "tensor", Y_RUN, axis_index_groups=along_y).reshape(-1, KV)

    pre_act = jnp.dot(task_embed, hyper_in, preferred_element_type=f32)
    hidden = jax.nn.silu(pre_act).astype(bf16)

    def chosen_by(which):
        ids = lax.dynamic_index_in_dim(
            task_ids.reshape(n_chips, CORES, SEQS), which, 1, keepdims=False
        ).reshape(n_chips * SEQS)
        hot = (ids[:, None] == jnp.arange(NTASK, dtype=jnp.int32)[None, :]).astype(bf16)
        return hot, jnp.dot(hot, hidden, preferred_element_type=f32).astype(bf16)

    heads = jnp.concatenate((head_a, head_b), axis=1)

    def terms_of(pick):
        return jnp.dot(pick, heads, preferred_element_type=f32)

    hot_mate, pick_mate = chosen_by(1 - core)
    hot_mine, pick_mine = chosen_by(core)
    from_mate = swapped(terms_of(pick_mate).astype(bf16), "dp", 1)
    run_zero = zero_after(cot_run).astype(bf16)
    terms = (terms_of(pick_mine + run_zero) + from_mate.astype(f32)).astype(bf16)
    term_width = down_width + up_width
    weight_own = value_weight.T.reshape(1, SEQS, -1)
    sent = jnp.concatenate(
        (
            terms.reshape(n_chips, SEQS, term_width),
            jnp.broadcast_to(weight_own, (n_chips,) + weight_own.shape[1:]),
        ),
        axis=2,
    )
    came = lax.all_to_all(sent, "dp", 0, 0, axis_index_groups=same_core)
    sums = jnp.sum(came[:, :, :term_width].astype(f32), axis=0)
    down_pick = (sums[:, :down_width] * (1.0 / math.sqrt(D))).astype(bf16)
    up_pick = (sums[:, down_width:] * (1.0 / math.sqrt(R))).astype(bf16)
    down_cat = down_pick.reshape(SEQS, width_own, R).transpose(1, 0, 2).reshape(width_own, ADA)

    place_x = place // Y_RUN
    cot_full = gathered(cot_run, place_x, n_x, Y_RUN)

    first, second = seq_lengths[0, 0], seq_lengths[0, 1]
    places = jnp.arange(rows_total, dtype=jnp.int32)[:, None]
    in_second = (places >= first) & (places < first + second)
    in_first = jnp.broadcast_to(places < first, (rows_total, R))
    col_mask = jnp.concatenate(
        (in_first, jnp.broadcast_to(in_second, (rows_total, R))), axis=1
    ).astype(f32)

    low_part = (jnp.dot(tokens, down_cat, preferred_element_type=f32) * col_mask).astype(bf16)
    up_part = lax.dot_general(cot_full, low_part, outer_dims, preferred_element_type=f32).astype(
        bf16
    )
    low_lines = rows_own * ADA // KV
    up_lines = outputs_own * ADA // KV
    pick_lines = SEQS * up_width // KV
    block = jnp.concatenate(
        (
            low_part.reshape(n_tensor, low_lines, KV),
            up_part.reshape(n_tensor, up_lines, KV),
            jnp.broadcast_to(up_pick.reshape(1, pick_lines, KV), (n_tensor, pick_lines, KV)),
        ),
        axis=1,
    )
    summed = low_lines + up_lines
    low_came = lax.all_to_all(block, "tensor", 0, 0)
    whole = jnp.sum(low_came[:, :summed].astype(f32), axis=0)
    low_rows = whole[:low_lines].reshape(rows_own, ADA)
    up_grad = whole[low_lines:].reshape(outputs_own, ADA)
    up_cat = (
        low_came[:, summed:]
        .reshape(n_tensor, SEQS, outputs_own, R)
        .transpose(0, 2, 1, 3)
        .reshape(KV, ADA)
    )

    weight_mine = came[:, :, term_width:]
    weight_mate = swapped(weight_mine, "dp", 1)
    weight_mine = weight_mine.reshape(n_chips, KV // n_dp, width_own)
    weight_mate = weight_mate.reshape(n_chips, KV // n_dp, width_own)
    weight_t = jnp.stack(
        (
            jnp.where(core == 0, weight_mine, weight_mate),
            jnp.where(core == 0, weight_mate, weight_mine),
        ),
        axis=1,
    ).reshape(KV, width_own)
    frozen_t = lax.dot_general(
        weight_t, tokens, inner_dims, preferred_element_type=f32
    ).astype(bf16)

    down_scale = 1.0 / math.sqrt(D)
    up_scale = 1.0 / math.sqrt(R)
    back_low = (jnp.dot(cot_full, up_cat, preferred_element_type=f32) * col_mask).astype(bf16)
    down_grad = down_scale * lax.dot_general(
        tokens, back_low, outer_dims, preferred_element_type=f32
    )
    up_grad = up_scale * up_grad
    down_seq = down_grad.reshape(width_own, SEQS, R).transpose(1, 0, 2).reshape(SEQS, down_width)
    up_seq = up_grad.reshape(outputs_own, SEQS, R).transpose(1, 0, 2).reshape(SEQS, up_width)
    own_grads = jnp.concatenate((down_seq, up_seq), axis=1).astype(bf16)
    grads_mine = spread(own_grads, "dp", n_chips, axis_index_groups=same_core)

    run_rows = Y_RUN * rows_own

    def run_of(x):
        return lax.dynamic_slice_in_dim(frozen_t, x * run_rows, run_rows, 1)

    frozen_kept = run_of(place_x)
    frozen_came = [
        swapped(run_of(place_x ^ step), "tensor", step * Y_RUN)
        for step in range(1, n_x)
    ]
    grads_mate = swapped(grads_mine, "dp", 1)

    def hidden_terms(grads, hot):
        part = lax.dot_general(
            grads.reshape(n_chips * SEQS, -1), heads, inner_dims, preferred_element_type=f32
        )
        return lax.dot_general(hot.astype(f32), part, outer_dims, precision=precise)

    by_task = hidden_terms(grads_mine, hot_mine) + hidden_terms(grads_mate, hot_mate)
    hidden_x = jnp.sum(
        spread(by_task.reshape(1, -1), "tensor", n_x, axis_index_groups=along_x), axis=0
    )

    task_zero = zero_after(by_task)
    rows_x = frozen_kept.astype(f32) + task_zero.astype(f32)
    for other in frozen_came:
        rows_x = rows_x + other.astype(f32)
    last = jnp.concatenate(
        (
            rows_x.astype(bf16).T.reshape(Y_RUN, rows_own, KV),
            jnp.broadcast_to(
                jnp.concatenate(parts_of(hidden_x), axis=0).reshape(1, -1, KV),
                (Y_RUN, 3 * hidden_x.size // KV, KV),
            ),
        ),
        axis=1,
    )
    last = jnp.sum(
        lax.all_to_all(last, "tensor", 0, 0, axis_index_groups=along_y).astype(f32), axis=0
    )
    frozen_rows = last[:rows_own]
    grad_hidden = jnp.sum(last[rows_own:].reshape((3,) + by_task.shape), axis=0)

    last_zero = zero_after(hidden_x).astype(bf16)

    adapter_back = lax.dot_general(back_low + task_zero.astype(bf16), down_cat, inner_dims, preferred_element_type=f32)
    frozen_back = jnp.dot(cot_full, weight_t, preferred_element_type=f32)
    grad_tokens = (frozen_back + last_zero.astype(f32) + adapter_back).astype(bf16)

    def head_grads(grads, pick):
        return lax.dot_general(
            pick + last_zero,
            grads.reshape(n_chips * SEQS, -1),
            outer_dims,
            preferred_element_type=f32,
        )

    grad_heads = head_grads(grads_mine, pick_mine) + head_grads(grads_mate, pick_mate)
    grad_head_a = grad_heads[:, :down_width]
    grad_head_b = grad_heads[:, down_width:]
    grad_pre = grad_hidden * silu_slope(pre_act)
    grad_hyper_in = lax.dot_general(
        task_embed.astype(f32), grad_pre, outer_dims, precision=precise
    )

    adapter = lax.dot_general(
        low_rows.astype(f32), up_cat.astype(f32), inner_dims, precision=precise
    )
    values = (frozen_rows + adapter).astype(bf16)
    return (values, grad_tokens, grad_head_a, grad_head_b, grad_hyper_in)


def solution(mesh):
    placed = (
        P("dp", "tensor"),
        P("tensor", "dp"),
        P("dp", None),
        P(),
        P(),
        P(None, "dp"),
        P("dp", "tensor"),
        P("dp", "tensor"),
        P(("dp", "tensor"), None),
    )
    return jax.shard_map(
        shards,
        mesh=mesh,
        in_specs=placed,
        out_specs=(
            P(("dp", "tensor"), None),
            P("dp", "tensor"),
            P("dp", "tensor"),
            P("dp", "tensor"),
            P(None, "dp"),
        ),
        check_vma=False,
    )
```

```python
import math

import jax
import jax.numpy as jnp
from jax import lax
from jax.sharding import PartitionSpec as P

D = 8192
KV = 512
R = 8
NTASK = 32
SEQS = 2
ADA = SEQS * R

precise = lax.Precision.HIGHEST
inner_dims = (((1,), (1,)), ((), ()))
outer_dims = (((0,), (0,)), ((), ()))
bf16 = jnp.bfloat16
f32 = jnp.float32

CORES = 2
Y_RUN = 4


def silu_slope(pre_act):
    sigma = jax.nn.sigmoid(pre_act)
    return sigma * (1.0 + pre_act * (1.0 - sigma))


def spread(block, axes, count, **kw):
    copies = jnp.broadcast_to(block[None], (count,) + block.shape)
    return lax.all_to_all(copies, axes, 0, 0, **kw)


def swapped(block, axis, distance):
    pairs = [(i, i ^ distance) for i in range(lax.axis_size(axis))]
    return lax.ppermute(block, axis, pairs)


def zero_after(value):
    first = value.reshape(-1)[0].astype(f32)
    return (jnp.floor(first) > first).astype(jnp.int32)


def parts_of(value):
    parts = []
    for _ in range(2):
        part = lax.reduce_precision(value, 8, 7)
        parts.append(part.astype(bf16))
        value = value - part
    return parts


def gathered(block, part, count, stride):
    every = jnp.zeros((count,) + block.shape, block.dtype)
    every = lax.dynamic_update_index_in_dim(every, block, part, 0)
    for step in range(1, count):
        other = swapped(block, "tensor", step * stride)
        every = lax.dynamic_update_index_in_dim(every, other, part ^ step, 0)
    return every.reshape((count * block.shape[0],) + block.shape[1:])


def shards(
    tokens, value_weight, seq_lengths, task_ids, task_embed, hyper_in, head_a, head_b, cotangent
):
    n_dp = lax.axis_size("dp")
    n_chips = n_dp // CORES
    n_tensor = lax.axis_size("tensor")
    n_x = n_tensor // Y_RUN
    rows_total, width_own = tokens.shape
    rows_own = rows_total // n_tensor
    outputs_own = KV // n_tensor
    down_width = width_own * R
    up_width = outputs_own * R
    along_y = [[x * Y_RUN + y for y in range(Y_RUN)] for x in range(n_x)]
    along_x = [[x * Y_RUN + y for x in range(n_x)] for y in range(Y_RUN)]
    same_core = [[chip * CORES + core for chip in range(n_chips)] for core in range(CORES)]
    core = lax.axis_index("dp") % CORES
    place = lax.axis_index("tensor")

    cot_run = spread(cotangent, "tensor", Y_RUN, axis_index_groups=along_y).reshape(-1, KV)

    pre_act = jnp.dot(task_embed, hyper_in, preferred_element_type=f32)
    hidden = jax.nn.silu(pre_act).astype(bf16)

    def chosen_by(which):
        ids = lax.dynamic_index_in_dim(
            task_ids.reshape(n_chips, CORES, SEQS), which, 1, keepdims=False
        ).reshape(n_chips * SEQS)
        hot = (ids[:, None] == jnp.arange(NTASK, dtype=jnp.int32)[None, :]).astype(bf16)
        return hot, jnp.dot(hot, hidden, preferred_element_type=f32).astype(bf16)

    heads = jnp.concatenate((head_a, head_b), axis=1)

    def terms_of(pick):
        return jnp.dot(pick, heads, preferred_element_type=f32)

    hot_mate, pick_mate = chosen_by(1 - core)
    hot_mine, pick_mine = chosen_by(core)
    from_mate = swapped(terms_of(pick_mate).astype(bf16), "dp", 1)
    run_zero = zero_after(cot_run).astype(bf16)
    terms = (terms_of(pick_mine + run_zero) + from_mate.astype(f32)).astype(bf16)
    term_width = down_width + up_width
    weight_own = value_weight.T.reshape(1, SEQS, -1)
    sent = jnp.concatenate(
        (
            terms.reshape(n_chips, SEQS, term_width),
            jnp.broadcast_to(weight_own, (n_chips,) + weight_own.shape[1:]),
        ),
        axis=2,
    )
    came = lax.all_to_all(sent, "dp", 0, 0, axis_index_groups=same_core)
    sums = jnp.sum(came[:, :, :term_width].astype(f32), axis=0)
    down_pick = (sums[:, :down_width] * (1.0 / math.sqrt(D))).astype(bf16)
    up_pick = (sums[:, down_width:] * (1.0 / math.sqrt(R))).astype(bf16)
    down_cat = down_pick.reshape(SEQS, width_own, R).transpose(1, 0, 2).reshape(width_own, ADA)

    place_x = place // Y_RUN
    cot_full = gathered(cot_run, place_x, n_x, Y_RUN)

    first, second = seq_lengths[0, 0], seq_lengths[0, 1]
    places = jnp.arange(rows_total, dtype=jnp.int32)[:, None]
    in_second = (places >= first) & (places < first + second)
    in_first = jnp.broadcast_to(places < first, (rows_total, R))
    col_mask = jnp.concatenate(
        (in_first, jnp.broadcast_to(in_second, (rows_total, R))), axis=1
    ).astype(f32)

    low_part = (jnp.dot(tokens, down_cat, preferred_element_type=f32) * col_mask).astype(bf16)
    up_part = lax.dot_general(cot_full, low_part, outer_dims, preferred_element_type=f32).astype(
        bf16
    )
    low_lines = rows_own * ADA // KV
    up_lines = outputs_own * ADA // KV
    pick_lines = SEQS * up_width // KV
    block = jnp.concatenate(
        (
            low_part.reshape(n_tensor, low_lines, KV),
            up_part.reshape(n_tensor, up_lines, KV),
            jnp.broadcast_to(up_pick.reshape(1, pick_lines, KV), (n_tensor, pick_lines, KV)),
        ),
        axis=1,
    )
    summed = low_lines + up_lines
    low_came = lax.all_to_all(block, "tensor", 0, 0)
    whole = jnp.sum(low_came[:, :summed].astype(f32), axis=0)
    low_rows = whole[:low_lines].reshape(rows_own, ADA)
    up_grad = whole[low_lines:].reshape(outputs_own, ADA)
    up_cat = (
        low_came[:, summed:]
        .reshape(n_tensor, SEQS, outputs_own, R)
        .transpose(0, 2, 1, 3)
        .reshape(KV, ADA)
    )

    weight_mine = came[:, :, term_width:]
    weight_mate = swapped(weight_mine, "dp", 1)
    weight_mine = weight_mine.reshape(n_chips, KV // n_dp, width_own)
    weight_mate = weight_mate.reshape(n_chips, KV // n_dp, width_own)
    weight_t = jnp.stack(
        (
            jnp.where(core == 0, weight_mine, weight_mate),
            jnp.where(core == 0, weight_mate, weight_mine),
        ),
        axis=1,
    ).reshape(KV, width_own)
    frozen_t = lax.dot_general(
        weight_t, tokens, inner_dims, preferred_element_type=f32
    ).astype(bf16)

    down_scale = 1.0 / math.sqrt(D)
    up_scale = 1.0 / math.sqrt(R)
    back_low = (jnp.dot(cot_full, up_cat, preferred_element_type=f32) * col_mask).astype(bf16)
    down_grad = down_scale * lax.dot_general(
        tokens, back_low, outer_dims, preferred_element_type=f32
    )
    up_grad = up_scale * up_grad
    down_seq = down_grad.reshape(width_own, SEQS, R).transpose(1, 0, 2).reshape(SEQS, down_width)
    up_seq = up_grad.reshape(outputs_own, SEQS, R).transpose(1, 0, 2).reshape(SEQS, up_width)
    own_grads = jnp.concatenate((down_seq, up_seq), axis=1).astype(bf16)
    grads_mine = spread(own_grads, "dp", n_chips, axis_index_groups=same_core)

    run_rows = Y_RUN * rows_own

    def run_of(x):
        return lax.dynamic_slice_in_dim(frozen_t, x * run_rows, run_rows, 1)

    frozen_kept = run_of(place_x)
    frozen_came = [
        swapped(run_of(place_x ^ step), "tensor", step * Y_RUN)
        for step in range(1, n_x)
    ]
    grads_mate = swapped(grads_mine, "dp", 1)

    def hidden_terms(grads, hot):
        part = lax.dot_general(
            grads.reshape(n_chips * SEQS, -1), heads, inner_dims, preferred_element_type=f32
        )
        return lax.dot_general(hot.astype(f32), part, outer_dims, precision=precise)

    by_task = hidden_terms(grads_mine, hot_mine) + hidden_terms(grads_mate, hot_mate)
    hidden_x = jnp.sum(
        spread(by_task.reshape(1, -1), "tensor", n_x, axis_index_groups=along_x), axis=0
    )

    task_zero = zero_after(grads_mate)
    rows_x = frozen_kept.astype(f32) + task_zero.astype(f32)
    for other in frozen_came:
        rows_x = rows_x + other.astype(f32)
    last = jnp.concatenate(
        (
            rows_x.astype(bf16).T.reshape(Y_RUN, rows_own, KV),
            jnp.broadcast_to(
                jnp.concatenate(parts_of(hidden_x), axis=0).reshape(1, -1, KV),
                (Y_RUN, 2 * hidden_x.size // KV, KV),
            ),
        ),
        axis=1,
    )
    last = jnp.sum(
        lax.all_to_all(last, "tensor", 0, 0, axis_index_groups=along_y).astype(f32), axis=0
    )
    frozen_rows = last[:rows_own]
    grad_hidden = jnp.sum(last[rows_own:].reshape((2,) + by_task.shape), axis=0)

    last_zero = zero_after(hidden_x).astype(bf16)

    adapter_back = lax.dot_general(back_low + task_zero.astype(bf16), down_cat, inner_dims, preferred_element_type=f32)
    frozen_back = jnp.dot(cot_full, weight_t, preferred_element_type=f32)
    grad_tokens = (frozen_back + last_zero.astype(f32) + adapter_back).astype(bf16)

    def head_grads(grads, pick):
        return lax.dot_general(
            pick + task_zero.astype(bf16),
            grads.reshape(n_chips * SEQS, -1),
            outer_dims,
            preferred_element_type=f32,
        )

    grad_heads = head_grads(grads_mine, pick_mine) + head_grads(grads_mate, pick_mate)
    grad_head_a = grad_heads[:, :down_width]
    grad_head_b = grad_heads[:, down_width:]
    grad_pre = grad_hidden * silu_slope(pre_act)
    grad_hyper_in = lax.dot_general(
        task_embed.astype(f32), grad_pre, outer_dims, precision=precise
    )

    adapter = lax.dot_general(
        low_rows.astype(f32), up_cat.astype(f32), inner_dims, precision=precise
    )
    values = (frozen_rows + adapter).astype(bf16)
    return (values, grad_tokens, grad_head_a, grad_head_b, grad_hyper_in)


def solution(mesh):
    placed = (
        P("dp", "tensor"),
        P("tensor", "dp"),
        P("dp", None),
        P(),
        P(),
        P(None, "dp"),
        P("dp", "tensor"),
        P("dp", "tensor"),
        P(("dp", "tensor"), None),
    )
    return jax.shard_map(
        shards,
        mesh=mesh,
        in_specs=placed,
        out_specs=(
            P(("dp", "tensor"), None),
            P("dp", "tensor"),
            P("dp", "tensor"),
            P("dp", "tensor"),
            P(None, "dp"),
        ),
        check_vma=False,
    )
```

```python
import math

import jax
import jax.numpy as jnp
from jax import lax
from jax.sharding import PartitionSpec as P

D = 8192
KV = 512
R = 8
NTASK = 32
SEQS = 2
ADA = SEQS * R

precise = lax.Precision.HIGHEST
inner_dims = (((1,), (1,)), ((), ()))
outer_dims = (((0,), (0,)), ((), ()))
bf16 = jnp.bfloat16
f32 = jnp.float32

CORES = 2
Y_RUN = 4


def silu_slope(pre_act):
    sigma = jax.nn.sigmoid(pre_act)
    return sigma * (1.0 + pre_act * (1.0 - sigma))


def spread(block, axes, count, **kw):
    copies = jnp.broadcast_to(block[None], (count,) + block.shape)
    return lax.all_to_all(copies, axes, 0, 0, **kw)


def swapped(block, axis, distance):
    pairs = [(i, i ^ distance) for i in range(lax.axis_size(axis))]
    return lax.ppermute(block, axis, pairs)


def zero_after(value):
    first = value.reshape(-1)[0].astype(f32)
    return (jnp.floor(first) > first).astype(jnp.int32)


def parts_of(value):
    parts = []
    for _ in range(2):
        part = lax.reduce_precision(value, 8, 7)
        parts.append(part.astype(bf16))
        value = value - part
    return parts


def gathered(block, part, count, stride):
    every = jnp.zeros((count,) + block.shape, block.dtype)
    every = lax.dynamic_update_index_in_dim(every, block, part, 0)
    others = [swapped(block, "tensor", step * stride) for step in range(1, count)]
    for step, other in enumerate(others, 1):
        every = lax.dynamic_update_index_in_dim(every, other, part ^ step, 0)
    return every.reshape((count * block.shape[0],) + block.shape[1:]), others[0]


def shards(
    tokens, value_weight, seq_lengths, task_ids, task_embed, hyper_in, head_a, head_b, cotangent
):
    n_dp = lax.axis_size("dp")
    n_chips = n_dp // CORES
    n_tensor = lax.axis_size("tensor")
    n_x = n_tensor // Y_RUN
    rows_total, width_own = tokens.shape
    rows_own = rows_total // n_tensor
    outputs_own = KV // n_tensor
    down_width = width_own * R
    up_width = outputs_own * R
    along_y = [[x * Y_RUN + y for y in range(Y_RUN)] for x in range(n_x)]
    along_x = [[x * Y_RUN + y for x in range(n_x)] for y in range(Y_RUN)]
    same_core = [[chip * CORES + core for chip in range(n_chips)] for core in range(CORES)]
    core = lax.axis_index("dp") % CORES
    place = lax.axis_index("tensor")

    cot_run = spread(cotangent, "tensor", Y_RUN, axis_index_groups=along_y).reshape(-1, KV)

    pre_act = jnp.dot(task_embed, hyper_in, preferred_element_type=f32)
    hidden = jax.nn.silu(pre_act).astype(bf16)

    def chosen_by(which):
        ids = lax.dynamic_index_in_dim(
            task_ids.reshape(n_chips, CORES, SEQS), which, 1, keepdims=False
        ).reshape(n_chips * SEQS)
        hot = (ids[:, None] == jnp.arange(NTASK, dtype=jnp.int32)[None, :]).astype(bf16)
        return hot, jnp.dot(hot, hidden, preferred_element_type=f32).astype(bf16)

    heads = jnp.concatenate((head_a, head_b), axis=1)

    def terms_of(pick):
        return jnp.dot(pick, heads, preferred_element_type=f32)

    hot_mate, pick_mate = chosen_by(1 - core)
    hot_mine, pick_mine = chosen_by(core)
    from_mate = swapped(terms_of(pick_mate).astype(bf16), "dp", 1)
    run_zero = zero_after(cot_run).astype(bf16)
    terms = (terms_of(pick_mine + run_zero) + from_mate.astype(f32)).astype(bf16)
    term_width = down_width + up_width
    weight_own = value_weight.T.reshape(1, SEQS, -1)
    sent = jnp.concatenate(
        (
            terms.reshape(n_chips, SEQS, term_width),
            jnp.broadcast_to(weight_own, (n_chips,) + weight_own.shape[1:]),
        ),
        axis=2,
    )
    came = lax.all_to_all(sent, "dp", 0, 0, axis_index_groups=same_core)
    sums = jnp.sum(came[:, :, :term_width].astype(f32), axis=0)
    down_pick = (sums[:, :down_width] * (1.0 / math.sqrt(D))).astype(bf16)
    up_pick = (sums[:, down_width:] * (1.0 / math.sqrt(R))).astype(bf16)
    down_cat = down_pick.reshape(SEQS, width_own, R).transpose(1, 0, 2).reshape(width_own, ADA)

    place_x = place // Y_RUN
    cot_full, cot_came = gathered(cot_run, place_x, n_x, Y_RUN)

    lengths = seq_lengths[0] + zero_after(cot_came)
    first, second = lengths[0], lengths[1]
    places = jnp.arange(rows_total, dtype=jnp.int32)[:, None]
    in_second = (places >= first) & (places < first + second)
    in_first = jnp.broadcast_to(places < first, (rows_total, R))
    col_mask = jnp.concatenate(
        (in_first, jnp.broadcast_to(in_second, (rows_total, R))), axis=1
    ).astype(f32)

    low_part = (jnp.dot(tokens, down_cat, preferred_element_type=f32) * col_mask).astype(bf16)
    up_part = lax.dot_general(cot_full, low_part, outer_dims, preferred_element_type=f32).astype(
        bf16
    )
    low_lines = rows_own * ADA // KV
    up_lines = outputs_own * ADA // KV
    pick_lines = SEQS * up_width // KV
    block = jnp.concatenate(
        (
            low_part.reshape(n_tensor, low_lines, KV),
            up_part.reshape(n_tensor, up_lines, KV),
            jnp.broadcast_to(up_pick.reshape(1, pick_lines, KV), (n_tensor, pick_lines, KV)),
        ),
        axis=1,
    )
    summed = low_lines + up_lines
    low_came = lax.all_to_all(block, "tensor", 0, 0)
    whole = jnp.sum(low_came[:, :summed].astype(f32), axis=0)
    low_rows = whole[:low_lines].reshape(rows_own, ADA)
    up_grad = whole[low_lines:].reshape(outputs_own, ADA)
    up_cat = (
        low_came[:, summed:]
        .reshape(n_tensor, SEQS, outputs_own, R)
        .transpose(0, 2, 1, 3)
        .reshape(KV, ADA)
    )

    weight_mine = came[:, :, term_width:].reshape(n_chips, KV // n_dp, width_own)
    weight_mate = swapped(weight_mine, "dp", 1)
    weight_t = jnp.stack(
        (
            jnp.where(core == 0, weight_mine, weight_mate),
            jnp.where(core == 0, weight_mate, weight_mine),
        ),
        axis=1,
    ).reshape(KV, width_own)
    frozen_t = lax.dot_general(
        weight_t, tokens, inner_dims, preferred_element_type=f32
    ).astype(bf16)

    down_scale = 1.0 / math.sqrt(D)
    up_scale = 1.0 / math.sqrt(R)
    back_low = (jnp.dot(cot_full, up_cat, preferred_element_type=f32) * col_mask).astype(bf16)
    down_grad = down_scale * lax.dot_general(
        tokens, back_low, outer_dims, preferred_element_type=f32
    )
    up_grad = up_scale * up_grad
    down_seq = down_grad.reshape(width_own, SEQS, R).transpose(1, 0, 2).reshape(SEQS, down_width)
    up_seq = up_grad.reshape(outputs_own, SEQS, R).transpose(1, 0, 2).reshape(SEQS, up_width)
    own_grads = jnp.concatenate((down_seq, up_seq), axis=1).astype(bf16)
    grads_mine = spread(own_grads, "dp", n_chips, axis_index_groups=same_core)

    run_rows = Y_RUN * rows_own

    def run_of(x):
        return lax.dynamic_slice_in_dim(frozen_t, x * run_rows, run_rows, 1)

    frozen_kept = run_of(place_x)
    frozen_came = [
        swapped(run_of(place_x ^ step), "tensor", step * Y_RUN)
        for step in range(1, n_x)
    ]
    grads_mate = swapped(grads_mine, "dp", 1)

    def hidden_terms(grads, hot):
        part = lax.dot_general(
            grads.reshape(n_chips * SEQS, -1), heads, inner_dims, preferred_element_type=f32
        )
        return lax.dot_general(hot.astype(f32), part, outer_dims, precision=precise)

    by_task = hidden_terms(grads_mine, hot_mine) + hidden_terms(grads_mate, hot_mate)
    hidden_x = jnp.sum(
        spread(by_task.reshape(1, -1), "tensor", n_x, axis_index_groups=along_x), axis=0
    )

    task_zero = zero_after(grads_mate)
    rows_x = frozen_kept.astype(f32) + task_zero.astype(f32)
    for other in frozen_came:
        rows_x = rows_x + other.astype(f32)
    last = jnp.concatenate(
        (
            rows_x.astype(bf16).T.reshape(Y_RUN, rows_own, KV),
            jnp.broadcast_to(
                jnp.concatenate(parts_of(hidden_x), axis=0).reshape(1, -1, KV),
                (Y_RUN, 2 * hidden_x.size // KV, KV),
            ),
        ),
        axis=1,
    )
    last = jnp.sum(
        lax.all_to_all(last, "tensor", 0, 0, axis_index_groups=along_y).astype(f32), axis=0
    )
    frozen_rows = last[:rows_own]
    grad_hidden = jnp.sum(last[rows_own:].reshape((2,) + by_task.shape), axis=0)

    last_zero = zero_after(hidden_x).astype(bf16)

    adapter_back = lax.dot_general(back_low + task_zero.astype(bf16), down_cat, inner_dims, preferred_element_type=f32)
    frozen_back = jnp.dot(cot_full, weight_t, preferred_element_type=f32)
    grad_tokens = (frozen_back + last_zero.astype(f32) + adapter_back).astype(bf16)

    def head_grads(grads, pick):
        return lax.dot_general(
            pick + task_zero.astype(bf16),
            grads.reshape(n_chips * SEQS, -1),
            outer_dims,
            preferred_element_type=f32,
        )

    grad_heads = head_grads(grads_mine, pick_mine) + head_grads(grads_mate, pick_mate)
    grad_head_a = grad_heads[:, :down_width]
    grad_head_b = grad_heads[:, down_width:]
    grad_pre = grad_hidden * silu_slope(pre_act)
    grad_hyper_in = lax.dot_general(
        task_embed.astype(f32), grad_pre, outer_dims, precision=precise
    )

    adapter = lax.dot_general(
        low_rows.astype(f32), up_cat.astype(f32), inner_dims, precision=precise
    )
    values = (frozen_rows + adapter).astype(bf16)
    return (values, grad_tokens, grad_head_a, grad_head_b, grad_hyper_in)


def solution(mesh):
    placed = (
        P("dp", "tensor"),
        P("tensor", "dp"),
        P("dp", None),
        P(),
        P(),
        P(None, "dp"),
        P("dp", "tensor"),
        P("dp", "tensor"),
        P(("dp", "tensor"), None),
    )
    return jax.shard_map(
        shards,
        mesh=mesh,
        in_specs=placed,
        out_specs=(
            P(("dp", "tensor"), None),
            P("dp", "tensor"),
            P("dp", "tensor"),
            P("dp", "tensor"),
            P(None, "dp"),
        ),
        check_vma=False,
    )
```

```python
import math

import jax
import jax.numpy as jnp
from jax import lax
from jax.sharding import PartitionSpec as P

D = 8192
KV = 512
R = 8
NTASK = 32
SEQS = 2
ADA = SEQS * R

precise = lax.Precision.HIGHEST
inner_dims = (((1,), (1,)), ((), ()))
outer_dims = (((0,), (0,)), ((), ()))
bf16 = jnp.bfloat16
f32 = jnp.float32

CORES = 2
Y_RUN = 4


def silu_slope(pre_act):
    sigma = jax.nn.sigmoid(pre_act)
    return sigma * (1.0 + pre_act * (1.0 - sigma))


def spread(block, axes, count, **kw):
    copies = jnp.broadcast_to(block[None], (count,) + block.shape)
    return lax.all_to_all(copies, axes, 0, 0, **kw)


def swapped(block, axis, distance):
    pairs = [(i, i ^ distance) for i in range(lax.axis_size(axis))]
    return lax.ppermute(block, axis, pairs)


def zero_after(value):
    first = value.reshape(-1)[0].astype(f32)
    return (jnp.floor(first) > first).astype(jnp.int32)


def parts_of(value):
    parts = []
    for _ in range(2):
        part = lax.reduce_precision(value, 8, 7)
        parts.append(part.astype(bf16))
        value = value - part
    return parts


def gathered(block, part, count, stride):
    every = jnp.zeros((count,) + block.shape, block.dtype)
    every = lax.dynamic_update_index_in_dim(every, block, part, 0)
    for step in range(1, count):
        other = swapped(block, "tensor", step * stride)
        every = lax.dynamic_update_index_in_dim(every, other, part ^ step, 0)
    return every.reshape((count * block.shape[0],) + block.shape[1:])


def shards(
    tokens, value_weight, seq_lengths, task_ids, task_embed, hyper_in, head_a, head_b, cotangent
):
    n_dp = lax.axis_size("dp")
    n_chips = n_dp // CORES
    n_tensor = lax.axis_size("tensor")
    n_x = n_tensor // Y_RUN
    rows_total, width_own = tokens.shape
    rows_own = rows_total // n_tensor
    outputs_own = KV // n_tensor
    down_width = width_own * R
    up_width = outputs_own * R
    along_y = [[x * Y_RUN + y for y in range(Y_RUN)] for x in range(n_x)]
    along_x = [[x * Y_RUN + y for x in range(n_x)] for y in range(Y_RUN)]
    same_core = [[chip * CORES + core for chip in range(n_chips)] for core in range(CORES)]
    core = lax.axis_index("dp") % CORES
    place = lax.axis_index("tensor")

    cot_run = spread(cotangent, "tensor", Y_RUN, axis_index_groups=along_y).reshape(-1, KV)

    pre_act = jnp.dot(task_embed, hyper_in, preferred_element_type=f32)
    hidden = jax.nn.silu(pre_act).astype(bf16)

    def chosen_by(which):
        ids = lax.dynamic_index_in_dim(
            task_ids.reshape(n_chips, CORES, SEQS), which, 1, keepdims=False
        ).reshape(n_chips * SEQS)
        hot = (ids[:, None] == jnp.arange(NTASK, dtype=jnp.int32)[None, :]).astype(bf16)
        return hot, jnp.dot(hot, hidden, preferred_element_type=f32).astype(bf16)

    heads = jnp.concatenate((head_a, head_b), axis=1)

    def terms_of(pick):
        return jnp.dot(pick, heads, preferred_element_type=f32)

    hot_mate, pick_mate = chosen_by(1 - core)
    hot_mine, pick_mine = chosen_by(core)
    from_mate = swapped(terms_of(pick_mate).astype(bf16), "dp", 1)
    run_zero = zero_after(cot_run).astype(bf16)
    terms = (terms_of(pick_mine + run_zero) + from_mate.astype(f32)).astype(bf16)
    term_width = down_width + up_width
    weight_own = value_weight.T.reshape(1, SEQS, -1)
    sent = jnp.concatenate(
        (
            terms.reshape(n_chips, SEQS, term_width),
            jnp.broadcast_to(weight_own, (n_chips,) + weight_own.shape[1:]),
        ),
        axis=2,
    )
    came = lax.all_to_all(sent, "dp", 0, 0, axis_index_groups=same_core)
    sums = jnp.sum(came[:, :, :term_width].astype(f32), axis=0)
    down_pick = (sums[:, :down_width] * (1.0 / math.sqrt(D))).astype(bf16)
    up_pick = (sums[:, down_width:] * (1.0 / math.sqrt(R))).astype(bf16)
    down_cat = down_pick.reshape(SEQS, width_own, R).transpose(1, 0, 2).reshape(width_own, ADA)

    place_x = place // Y_RUN
    cot_full = gathered(cot_run, place_x, n_x, Y_RUN)

    first, second = seq_lengths[0, 0], seq_lengths[0, 1]
    places = jnp.arange(rows_total, dtype=jnp.int32)[:, None]
    in_second = (places >= first) & (places < first + second)
    in_first = jnp.broadcast_to(places < first, (rows_total, R))
    col_mask = jnp.concatenate(
        (in_first, jnp.broadcast_to(in_second, (rows_total, R))), axis=1
    ).astype(f32)

    low_part = (jnp.dot(tokens, down_cat, preferred_element_type=f32) * col_mask).astype(bf16)
    up_part = lax.dot_general(cot_full, low_part, outer_dims, preferred_element_type=f32).astype(
        bf16
    )
    low_lines = rows_own * ADA // KV
    up_lines = outputs_own * ADA // KV
    pick_lines = SEQS * up_width // KV
    block = jnp.concatenate(
        (
            low_part.reshape(n_tensor, low_lines, KV),
            up_part.reshape(n_tensor, up_lines, KV),
            jnp.broadcast_to(up_pick.reshape(1, pick_lines, KV), (n_tensor, pick_lines, KV)),
        ),
        axis=1,
    )
    summed = low_lines + up_lines
    low_came = lax.all_to_all(block, "tensor", 0, 0)
    whole = jnp.sum(low_came[:, :summed].astype(f32), axis=0)
    low_rows = whole[:low_lines].reshape(rows_own, ADA)
    up_grad = whole[low_lines:].reshape(outputs_own, ADA)
    up_cat = (
        low_came[:, summed:]
        .reshape(n_tensor, SEQS, outputs_own, R)
        .transpose(0, 2, 1, 3)
        .reshape(KV, ADA)
    )

    weight_mine = came[:, :, term_width:].reshape(n_chips, KV // n_dp, width_own)
    weight_mate = swapped(weight_mine, "dp", 1)
    weight_t = jnp.stack(
        (
            jnp.where(core == 0, weight_mine, weight_mate),
            jnp.where(core == 0, weight_mate, weight_mine),
        ),
        axis=1,
    ).reshape(KV, width_own)
    frozen_t = lax.dot_general(
        weight_t, tokens, inner_dims, preferred_element_type=f32
    ).astype(bf16)

    down_scale = 1.0 / math.sqrt(D)
    up_scale = 1.0 / math.sqrt(R)
    back_low = (jnp.dot(cot_full, up_cat, preferred_element_type=f32) * col_mask).astype(bf16)
    down_grad = down_scale * lax.dot_general(
        tokens, back_low, outer_dims, preferred_element_type=f32
    )
    up_grad = up_scale * up_grad
    down_seq = down_grad.reshape(width_own, SEQS, R).transpose(1, 0, 2).reshape(SEQS, down_width)
    up_seq = up_grad.reshape(outputs_own, SEQS, R).transpose(1, 0, 2).reshape(SEQS, up_width)
    own_grads = jnp.concatenate((down_seq, up_seq), axis=1).astype(bf16)
    grads_mine = spread(own_grads, "dp", n_chips, axis_index_groups=same_core)

    run_rows = Y_RUN * rows_own

    def run_of(x):
        return lax.dynamic_slice_in_dim(frozen_t, x * run_rows, run_rows, 1)

    frozen_kept = run_of(place_x)
    frozen_came = [
        swapped(run_of(place_x ^ step), "tensor", step * Y_RUN)
        for step in range(1, n_x)
    ]
    grads_mate = swapped(grads_mine, "dp", 1)

    def hidden_terms(grads, hot):
        part = lax.dot_general(
            grads.reshape(n_chips * SEQS, -1), heads, inner_dims, preferred_element_type=f32
        )
        return lax.dot_general(hot.astype(f32), part, outer_dims, precision=precise)

    by_task = hidden_terms(grads_mine, hot_mine) + hidden_terms(grads_mate, hot_mate)
    hidden_x = jnp.sum(
        spread(by_task.reshape(1, -1), "tensor", n_x, axis_index_groups=along_x), axis=0
    )

    task_zero = zero_after(grads_mate)
    rows_x = frozen_kept.astype(f32) + task_zero.astype(f32)
    for other in frozen_came:
        rows_x = rows_x + other.astype(f32)
    last = jnp.concatenate(
        (
            rows_x.astype(bf16).T.reshape(Y_RUN, rows_own, KV),
            jnp.broadcast_to(
                jnp.concatenate(parts_of(hidden_x), axis=0).reshape(1, -1, KV),
                (Y_RUN, 2 * hidden_x.size // KV, KV),
            ),
        ),
        axis=1,
    )
    last = jnp.sum(
        lax.all_to_all(last, "tensor", 0, 0, axis_index_groups=along_y).astype(f32), axis=0
    )
    frozen_rows = last[:rows_own]
    grad_hidden = jnp.sum(last[rows_own:].reshape((2,) + by_task.shape), axis=0)

    last_zero = zero_after(hidden_x).astype(bf16)

    adapter_back = lax.dot_general(back_low + task_zero.astype(bf16), down_cat, inner_dims, preferred_element_type=f32)
    frozen_back = jnp.dot(cot_full, weight_t, preferred_element_type=f32)
    grad_tokens = (frozen_back + last_zero.astype(f32) + adapter_back).astype(bf16)

    def head_grads(grads, pick):
        return lax.dot_general(
            pick + task_zero.astype(bf16),
            grads.reshape(n_chips * SEQS, -1),
            outer_dims,
            preferred_element_type=f32,
        )

    grad_heads = head_grads(grads_mine, pick_mine) + head_grads(grads_mate, pick_mate)
    grad_head_a = grad_heads[:, :down_width]
    grad_head_b = grad_heads[:, down_width:]
    grad_pre = grad_hidden * silu_slope(pre_act)
    grad_hyper_in = lax.dot_general(
        task_embed.astype(f32), grad_pre, outer_dims, precision=precise
    )

    adapter = lax.dot_general(
        low_rows.astype(f32), up_cat.astype(f32), inner_dims, precision=precise
    )
    values = (frozen_rows + adapter).astype(bf16)
    return (values, grad_tokens, grad_head_a, grad_head_b, grad_hyper_in)


def solution(mesh):
    placed = (
        P("dp", "tensor"),
        P("tensor", "dp"),
        P("dp", None),
        P(),
        P(),
        P(None, "dp"),
        P("dp", "tensor"),
        P("dp", "tensor"),
        P(("dp", "tensor"), None),
    )
    return jax.shard_map(
        shards,
        mesh=mesh,
        in_specs=placed,
        out_specs=(
            P(("dp", "tensor"), None),
            P("dp", "tensor"),
            P("dp", "tensor"),
            P("dp", "tensor"),
            P(None, "dp"),
        ),
        check_vma=False,
    )
```

```python
import math

import jax
import jax.numpy as jnp
from jax import lax
from jax.sharding import PartitionSpec as P

D = 8192
KV = 512
R = 8
NTASK = 32
SEQS = 2
ADA = SEQS * R

precise = lax.Precision.HIGHEST
inner_dims = (((1,), (1,)), ((), ()))
outer_dims = (((0,), (0,)), ((), ()))
bf16 = jnp.bfloat16
f32 = jnp.float32

CORES = 2
Y_RUN = 4


def silu_slope(pre_act):
    sigma = jax.nn.sigmoid(pre_act)
    return sigma * (1.0 + pre_act * (1.0 - sigma))


def spread(block, axes, count, **kw):
    copies = jnp.broadcast_to(block[None], (count,) + block.shape)
    return lax.all_to_all(copies, axes, 0, 0, **kw)


def swapped(block, axis, distance):
    pairs = [(i, i ^ distance) for i in range(lax.axis_size(axis))]
    return lax.ppermute(block, axis, pairs)


def zero_after(value):
    first = value.reshape(-1)[0].astype(f32)
    return (jnp.floor(first) > first).astype(jnp.int32)


def parts_of(value):
    parts = []
    for _ in range(2):
        part = lax.reduce_precision(value, 8, 7)
        parts.append(part.astype(bf16))
        value = value - part
    return parts


def gathered(block, part, count, stride):
    every = jnp.zeros((count,) + block.shape, block.dtype)
    every = lax.dynamic_update_index_in_dim(every, block, part, 0)
    for step in range(1, count):
        other = swapped(block, "tensor", step * stride)
        every = lax.dynamic_update_index_in_dim(every, other, part ^ step, 0)
    return every.reshape((count * block.shape[0],) + block.shape[1:])


def shards(
    tokens, value_weight, seq_lengths, task_ids, task_embed, hyper_in, head_a, head_b, cotangent
):
    n_dp = lax.axis_size("dp")
    n_chips = n_dp // CORES
    n_tensor = lax.axis_size("tensor")
    n_x = n_tensor // Y_RUN
    rows_total, width_own = tokens.shape
    rows_own = rows_total // n_tensor
    outputs_own = KV // n_tensor
    down_width = width_own * R
    up_width = outputs_own * R
    along_y = [[x * Y_RUN + y for y in range(Y_RUN)] for x in range(n_x)]
    along_x = [[x * Y_RUN + y for x in range(n_x)] for y in range(Y_RUN)]
    same_core = [[chip * CORES + core for chip in range(n_chips)] for core in range(CORES)]
    core = lax.axis_index("dp") % CORES
    place = lax.axis_index("tensor")

    cot_run = spread(cotangent, "tensor", Y_RUN, axis_index_groups=along_y).reshape(-1, KV)

    pre_act = jnp.dot(task_embed, hyper_in, preferred_element_type=f32)
    hidden = jax.nn.silu(pre_act).astype(bf16)

    def chosen_by(which):
        ids = lax.dynamic_index_in_dim(
            task_ids.reshape(n_chips, CORES, SEQS), which, 1, keepdims=False
        ).reshape(n_chips * SEQS)
        hot = (ids[:, None] == jnp.arange(NTASK, dtype=jnp.int32)[None, :]).astype(bf16)
        return hot, jnp.dot(hot, hidden, preferred_element_type=f32).astype(bf16)

    heads = jnp.concatenate((head_a, head_b), axis=1)

    def terms_of(pick):
        return jnp.dot(pick, heads, preferred_element_type=f32)

    hot_mate, pick_mate = chosen_by(1 - core)
    hot_mine, pick_mine = chosen_by(core)
    from_mate = swapped(terms_of(pick_mate).astype(bf16), "dp", 1)
    run_zero = zero_after(cot_run).astype(bf16)
    terms = (terms_of(pick_mine + run_zero) + from_mate.astype(f32)).astype(bf16)
    term_width = down_width + up_width
    weight_own = value_weight.T.reshape(1, SEQS, -1)
    sent = jnp.concatenate(
        (
            terms.reshape(n_chips, SEQS, term_width),
            jnp.broadcast_to(weight_own, (n_chips,) + weight_own.shape[1:]),
        ),
        axis=2,
    )
    came = lax.all_to_all(sent, "dp", 0, 0, axis_index_groups=same_core)
    sums = jnp.sum(came[:, :, :term_width].astype(f32), axis=0)
    down_pick = (sums[:, :down_width] * (1.0 / math.sqrt(D))).astype(bf16)
    up_pick = (sums[:, down_width:] * (1.0 / math.sqrt(R))).astype(bf16)
    down_cat = down_pick.reshape(SEQS, width_own, R).transpose(1, 0, 2).reshape(width_own, ADA)

    place_x = place // Y_RUN
    cot_full = gathered(cot_run, place_x, n_x, Y_RUN)

    first = seq_lengths[:, :1]
    both = first + seq_lengths[:, 1:2]
    places = jnp.arange(rows_total, dtype=jnp.int32)[:, None]
    column = jnp.arange(ADA, dtype=jnp.int32)[None, :]
    in_first = places < first
    inside = jnp.where(column < R, in_first, (places < both) & ~in_first)
    col_mask = inside.astype(f32)

    low_part = (jnp.dot(tokens, down_cat, preferred_element_type=f32) * col_mask).astype(bf16)
    up_part = lax.dot_general(cot_full, low_part, outer_dims, preferred_element_type=f32).astype(
        bf16
    )
    low_lines = rows_own * ADA // KV
    up_lines = outputs_own * ADA // KV
    pick_lines = SEQS * up_width // KV
    block = jnp.concatenate(
        (
            low_part.reshape(n_tensor, low_lines, KV),
            up_part.reshape(n_tensor, up_lines, KV),
            jnp.broadcast_to(up_pick.reshape(1, pick_lines, KV), (n_tensor, pick_lines, KV)),
        ),
        axis=1,
    )
    summed = low_lines + up_lines
    low_came = lax.all_to_all(block, "tensor", 0, 0)
    whole = jnp.sum(low_came[:, :summed].astype(f32), axis=0)
    low_rows = whole[:low_lines].reshape(rows_own, ADA)
    up_grad = whole[low_lines:].reshape(outputs_own, ADA)
    up_cat = (
        low_came[:, summed:]
        .reshape(n_tensor, SEQS, outputs_own, R)
        .transpose(0, 2, 1, 3)
        .reshape(KV, ADA)
    )

    weight_mine = came[:, :, term_width:].reshape(n_chips, KV // n_dp, width_own)
    weight_mate = swapped(weight_mine, "dp", 1)
    weight_t = jnp.stack(
        (
            jnp.where(core == 0, weight_mine, weight_mate),
            jnp.where(core == 0, weight_mate, weight_mine),
        ),
        axis=1,
    ).reshape(KV, width_own)
    frozen_t = lax.dot_general(
        weight_t, tokens, inner_dims, preferred_element_type=f32
    ).astype(bf16)

    down_scale = 1.0 / math.sqrt(D)
    up_scale = 1.0 / math.sqrt(R)
    back_low = (jnp.dot(cot_full, up_cat, preferred_element_type=f32) * col_mask).astype(bf16)
    down_grad = down_scale * lax.dot_general(
        tokens, back_low, outer_dims, preferred_element_type=f32
    )
    up_grad = up_scale * up_grad
    down_seq = down_grad.reshape(width_own, SEQS, R).transpose(1, 0, 2).reshape(SEQS, down_width)
    up_seq = up_grad.reshape(outputs_own, SEQS, R).transpose(1, 0, 2).reshape(SEQS, up_width)
    own_grads = jnp.concatenate((down_seq, up_seq), axis=1).astype(bf16)
    grads_mine = spread(own_grads, "dp", n_chips, axis_index_groups=same_core)

    run_rows = Y_RUN * rows_own

    def run_of(x):
        return lax.dynamic_slice_in_dim(frozen_t, x * run_rows, run_rows, 1)

    frozen_kept = run_of(place_x)
    frozen_came = [
        swapped(run_of(place_x ^ step), "tensor", step * Y_RUN)
        for step in range(1, n_x)
    ]
    grads_mate = swapped(grads_mine, "dp", 1)

    def hidden_terms(grads, hot):
        part = lax.dot_general(
            grads.reshape(n_chips * SEQS, -1), heads, inner_dims, preferred_element_type=f32
        )
        return lax.dot_general(hot.astype(f32), part, outer_dims, precision=precise)

    by_task = hidden_terms(grads_mine, hot_mine) + hidden_terms(grads_mate, hot_mate)
    hidden_x = jnp.sum(
        spread(by_task.reshape(1, -1), "tensor", n_x, axis_index_groups=along_x), axis=0
    )

    task_zero = zero_after(grads_mate)
    rows_x = frozen_kept.astype(f32) + task_zero.astype(f32)
    for other in frozen_came:
        rows_x = rows_x + other.astype(f32)
    last = jnp.concatenate(
        (
            rows_x.astype(bf16).T.reshape(Y_RUN, rows_own, KV),
            jnp.broadcast_to(
                jnp.concatenate(parts_of(hidden_x), axis=0).reshape(1, -1, KV),
                (Y_RUN, 2 * hidden_x.size // KV, KV),
            ),
        ),
        axis=1,
    )
    last = jnp.sum(
        lax.all_to_all(last, "tensor", 0, 0, axis_index_groups=along_y).astype(f32), axis=0
    )
    frozen_rows = last[:rows_own]
    grad_hidden = jnp.sum(last[rows_own:].reshape((2,) + by_task.shape), axis=0)

    last_zero = zero_after(hidden_x).astype(bf16)

    adapter_back = lax.dot_general(back_low + task_zero.astype(bf16), down_cat, inner_dims, preferred_element_type=f32)
    frozen_back = jnp.dot(cot_full, weight_t, preferred_element_type=f32)
    grad_tokens = (frozen_back + last_zero.astype(f32) + adapter_back).astype(bf16)

    def head_grads(grads, pick):
        return lax.dot_general(
            pick + task_zero.astype(bf16),
            grads.reshape(n_chips * SEQS, -1),
            outer_dims,
            preferred_element_type=f32,
        )

    grad_heads = head_grads(grads_mine, pick_mine) + head_grads(grads_mate, pick_mate)
    grad_head_a = grad_heads[:, :down_width]
    grad_head_b = grad_heads[:, down_width:]
    grad_pre = grad_hidden * silu_slope(pre_act)
    grad_hyper_in = lax.dot_general(
        task_embed.astype(f32), grad_pre, outer_dims, precision=precise
    )

    adapter = lax.dot_general(
        low_rows.astype(f32), up_cat.astype(f32), inner_dims, precision=precise
    )
    values = (frozen_rows + adapter).astype(bf16)
    return (values, grad_tokens, grad_head_a, grad_head_b, grad_hyper_in)


def solution(mesh):
    placed = (
        P("dp", "tensor"),
        P("tensor", "dp"),
        P("dp", None),
        P(),
        P(),
        P(None, "dp"),
        P("dp", "tensor"),
        P("dp", "tensor"),
        P(("dp", "tensor"), None),
    )
    return jax.shard_map(
        shards,
        mesh=mesh,
        in_specs=placed,
        out_specs=(
            P(("dp", "tensor"), None),
            P("dp", "tensor"),
            P("dp", "tensor"),
            P("dp", "tensor"),
            P(None, "dp"),
        ),
        check_vma=False,
    )
```

```python
import math

import jax
import jax.numpy as jnp
from jax import lax
from jax.sharding import PartitionSpec as P

D = 8192
KV = 512
R = 8
NTASK = 32
SEQS = 2
ADA = SEQS * R

precise = lax.Precision.HIGHEST
inner_dims = (((1,), (1,)), ((), ()))
outer_dims = (((0,), (0,)), ((), ()))
bf16 = jnp.bfloat16
f32 = jnp.float32

CORES = 2
Y_RUN = 4


def silu_slope(pre_act):
    sigma = jax.nn.sigmoid(pre_act)
    return sigma * (1.0 + pre_act * (1.0 - sigma))


def spread(block, axes, count, **kw):
    copies = jnp.broadcast_to(block[None], (count,) + block.shape)
    return lax.all_to_all(copies, axes, 0, 0, **kw)


def swapped(block, axis, distance):
    pairs = [(i, i ^ distance) for i in range(lax.axis_size(axis))]
    return lax.ppermute(block, axis, pairs)


def zero_after(value):
    first = value.reshape(-1)[0].astype(f32)
    return (jnp.floor(first) > first).astype(jnp.int32)


def parts_of(value):
    parts = []
    for _ in range(2):
        part = lax.reduce_precision(value, 8, 7)
        parts.append(part.astype(bf16))
        value = value - part
    return parts


def gathered(block, part, count, stride):
    every = jnp.zeros((count,) + block.shape, block.dtype)
    every = lax.dynamic_update_index_in_dim(every, block, part, 0)
    for step in range(1, count):
        other = swapped(block, "tensor", step * stride)
        every = lax.dynamic_update_index_in_dim(every, other, part ^ step, 0)
    return every.reshape((count * block.shape[0],) + block.shape[1:])


def shards(
    tokens, value_weight, seq_lengths, task_ids, task_embed, hyper_in, head_a, head_b, cotangent
):
    n_dp = lax.axis_size("dp")
    n_chips = n_dp // CORES
    n_tensor = lax.axis_size("tensor")
    n_x = n_tensor // Y_RUN
    rows_total, width_own = tokens.shape
    rows_own = rows_total // n_tensor
    outputs_own = KV // n_tensor
    down_width = width_own * R
    up_width = outputs_own * R
    along_y = [[x * Y_RUN + y for y in range(Y_RUN)] for x in range(n_x)]
    along_x = [[x * Y_RUN + y for x in range(n_x)] for y in range(Y_RUN)]
    same_core = [[chip * CORES + core for chip in range(n_chips)] for core in range(CORES)]
    core = lax.axis_index("dp") % CORES
    place = lax.axis_index("tensor")

    cot_run = spread(cotangent, "tensor", Y_RUN, axis_index_groups=along_y).reshape(-1, KV)

    pre_act = jnp.dot(task_embed, hyper_in, preferred_element_type=f32)
    hidden = jax.nn.silu(pre_act).astype(bf16)

    def chosen_by(which):
        ids = lax.dynamic_index_in_dim(
            task_ids.reshape(n_chips, CORES, SEQS), which, 1, keepdims=False
        ).reshape(n_chips * SEQS)
        hot = (ids[:, None] == jnp.arange(NTASK, dtype=jnp.int32)[None, :]).astype(bf16)
        return hot, jnp.dot(hot, hidden, preferred_element_type=f32).astype(bf16)

    heads = jnp.concatenate((head_a, head_b), axis=1)

    def terms_of(pick):
        return jnp.dot(pick, heads, preferred_element_type=f32)

    hot_mate, pick_mate = chosen_by(1 - core)
    hot_mine, pick_mine = chosen_by(core)
    from_mate = swapped(terms_of(pick_mate).astype(bf16), "dp", 1)
    run_zero = zero_after(cot_run).astype(bf16)
    terms = (terms_of(pick_mine + run_zero) + from_mate.astype(f32)).astype(bf16)
    term_width = down_width + up_width
    weight_own = value_weight.T.reshape(1, SEQS, -1)
    sent = jnp.concatenate(
        (
            terms.reshape(n_chips, SEQS, term_width),
            jnp.broadcast_to(weight_own, (n_chips,) + weight_own.shape[1:]),
        ),
        axis=2,
    )
    came = lax.all_to_all(sent, "dp", 0, 0, axis_index_groups=same_core)
    sums = jnp.sum(came[:, :, :term_width].astype(f32), axis=0)
    down_pick = (sums[:, :down_width] * (1.0 / math.sqrt(D))).astype(bf16)
    up_pick = (sums[:, down_width:] * (1.0 / math.sqrt(R))).astype(bf16)
    down_cat = down_pick.reshape(SEQS, width_own, R).transpose(1, 0, 2).reshape(width_own, ADA)

    place_x = place // Y_RUN
    cot_full = gathered(cot_run, place_x, n_x, Y_RUN)

    first, second = seq_lengths[0, 0], seq_lengths[0, 1]
    places = jnp.arange(rows_total, dtype=jnp.int32)[:, None]
    in_second = (places >= first) & (places < first + second)
    in_first = jnp.broadcast_to(places < first, (rows_total, R))
    col_mask = jnp.concatenate(
        (in_first, jnp.broadcast_to(in_second, (rows_total, R))), axis=1
    ).astype(f32)

    low_part = (jnp.dot(tokens, down_cat, preferred_element_type=f32) * col_mask).astype(bf16)
    up_part = lax.dot_general(cot_full, low_part, outer_dims, preferred_element_type=f32).astype(
        bf16
    )
    low_lines = rows_own * ADA // KV
    up_lines = outputs_own * ADA // KV
    pick_lines = SEQS * up_width // KV
    block = jnp.concatenate(
        (
            low_part.reshape(n_tensor, low_lines, KV),
            up_part.reshape(n_tensor, up_lines, KV),
            jnp.broadcast_to(up_pick.reshape(1, pick_lines, KV), (n_tensor, pick_lines, KV)),
        ),
        axis=1,
    )
    summed = low_lines + up_lines
    low_came = lax.all_to_all(block, "tensor", 0, 0)
    whole = jnp.sum(low_came[:, :summed].astype(f32), axis=0)
    low_rows = whole[:low_lines].reshape(rows_own, ADA)
    up_grad = whole[low_lines:].reshape(outputs_own, ADA)
    up_cat = (
        low_came[:, summed:]
        .reshape(n_tensor, SEQS, outputs_own, R)
        .transpose(0, 2, 1, 3)
        .reshape(KV, ADA)
    )

    weight_mine = came[:, :, term_width:].reshape(n_chips, KV // n_dp, width_own)
    weight_mate = swapped(weight_mine, "dp", 1)
    weight_t = jnp.stack(
        (
            jnp.where(core == 0, weight_mine, weight_mate),
            jnp.where(core == 0, weight_mate, weight_mine),
        ),
        axis=1,
    ).reshape(KV, width_own)
    frozen_t = lax.dot_general(
        weight_t, tokens, inner_dims, preferred_element_type=f32
    ).astype(bf16)

    down_scale = 1.0 / math.sqrt(D)
    up_scale = 1.0 / math.sqrt(R)
    back_low = (jnp.dot(cot_full, up_cat, preferred_element_type=f32) * col_mask).astype(bf16)
    down_grad = down_scale * lax.dot_general(
        tokens, back_low, outer_dims, preferred_element_type=f32
    )
    up_grad = up_scale * up_grad
    down_seq = down_grad.reshape(width_own, SEQS, R).transpose(1, 0, 2).reshape(SEQS, down_width)
    up_seq = up_grad.reshape(outputs_own, SEQS, R).transpose(1, 0, 2).reshape(SEQS, up_width)
    own_grads = jnp.concatenate((down_seq, up_seq), axis=1).astype(bf16)
    grads_mine = spread(own_grads, "dp", n_chips, axis_index_groups=same_core)

    run_rows = Y_RUN * rows_own

    def run_of(x):
        return lax.dynamic_slice_in_dim(frozen_t, x * run_rows, run_rows, 1)

    frozen_kept = run_of(place_x)
    frozen_came = [
        swapped(run_of(place_x ^ step), "tensor", step * Y_RUN)
        for step in (2, 3, 1)
    ]
    grads_mate = swapped(grads_mine, "dp", 1)

    def hidden_terms(grads, hot):
        part = lax.dot_general(
            grads.reshape(n_chips * SEQS, -1), heads, inner_dims, preferred_element_type=f32
        )
        return lax.dot_general(hot.astype(f32), part, outer_dims, precision=precise)

    by_task = hidden_terms(grads_mine, hot_mine) + hidden_terms(grads_mate, hot_mate)
    hidden_x = jnp.sum(
        spread(by_task.reshape(1, -1), "tensor", n_x, axis_index_groups=along_x), axis=0
    )

    task_zero = zero_after(grads_mate)
    rows_x = frozen_kept.astype(f32) + task_zero.astype(f32)
    for other in frozen_came:
        rows_x = rows_x + other.astype(f32)
    last = jnp.concatenate(
        (
            rows_x.astype(bf16).T.reshape(Y_RUN, rows_own, KV),
            jnp.broadcast_to(
                jnp.concatenate(parts_of(hidden_x), axis=0).reshape(1, -1, KV),
                (Y_RUN, 2 * hidden_x.size // KV, KV),
            ),
        ),
        axis=1,
    )
    last = jnp.sum(
        lax.all_to_all(last, "tensor", 0, 0, axis_index_groups=along_y).astype(f32), axis=0
    )
    frozen_rows = last[:rows_own]
    grad_hidden = jnp.sum(last[rows_own:].reshape((2,) + by_task.shape), axis=0)

    last_zero = zero_after(hidden_x).astype(bf16)

    adapter_back = lax.dot_general(back_low + task_zero.astype(bf16), down_cat, inner_dims, preferred_element_type=f32)
    frozen_back = jnp.dot(cot_full, weight_t, preferred_element_type=f32)
    grad_tokens = (frozen_back + last_zero.astype(f32) + adapter_back).astype(bf16)

    def head_grads(grads, pick):
        return lax.dot_general(
            pick + task_zero.astype(bf16),
            grads.reshape(n_chips * SEQS, -1),
            outer_dims,
            preferred_element_type=f32,
        )

    grad_heads = head_grads(grads_mine, pick_mine) + head_grads(grads_mate, pick_mate)
    grad_head_a = grad_heads[:, :down_width]
    grad_head_b = grad_heads[:, down_width:]
    grad_pre = grad_hidden * silu_slope(pre_act)
    grad_hyper_in = lax.dot_general(
        task_embed.astype(f32), grad_pre, outer_dims, precision=precise
    )

    adapter = lax.dot_general(
        low_rows.astype(f32), up_cat.astype(f32), inner_dims, precision=precise
    )
    values = (frozen_rows + adapter).astype(bf16)
    return (values, grad_tokens, grad_head_a, grad_head_b, grad_hyper_in)


def solution(mesh):
    placed = (
        P("dp", "tensor"),
        P("tensor", "dp"),
        P("dp", None),
        P(),
        P(),
        P(None, "dp"),
        P("dp", "tensor"),
        P("dp", "tensor"),
        P(("dp", "tensor"), None),
    )
    return jax.shard_map(
        shards,
        mesh=mesh,
        in_specs=placed,
        out_specs=(
            P(("dp", "tensor"), None),
            P("dp", "tensor"),
            P("dp", "tensor"),
            P("dp", "tensor"),
            P(None, "dp"),
        ),
        check_vma=False,
    )
```
